512 devices in a mesh: dp: 64 (over x, y, core), tensor: 8 (over z).
Axes of the slice: x: 4, y: 8, z: 8, core: 2. Of those that a mesh axis runs over, the one named last changes fastest.
Arguments:
- queries: bfloat16 [8192, 8192], P('dp', 'tensor'), may hold values from -52 to 52
- keys_in: bfloat16 [8192, 16, 1024], P('dp', 'tensor'), may hold values from -6.5 to 6.5
- values_in: bfloat16 [8192, 16, 1024], P('dp', 'tensor'), may hold values from -4 to 4
- dout: bfloat16 [8192, 8192], P('dp', 'tensor'), may hold values from -4 to 4
- req_tiles: int32 [8192], P('dp'), may hold values from 0 to 8191, as said below
- tile_docs: int32 [8192], P('dp'), may hold values from 0 to 7, as said below
- tile_rows: int32 [8192], P('dp'), may hold values from 0 to 127, as said below
- doc_ends: int32 [512], P('dp'), may hold values from 1 to 128, as said below
Outputs:
- grad_queries: bfloat16 [8192, 8192], P('dp', 'tensor')
- grad_keys: bfloat16 [8192, 16, 1024], P('dp', 'tensor')
- grad_values: bfloat16 [8192, 16, 1024], P('dp', 'tensor')
The draws below stay inside these ranges and needn't reach their ends.
Inputs may be any that keep to these rules, and one draw needn't show every extreme that they name: `req_tiles`: every tile id appears exactly once over all lists; tile g is held at index g // 128 of dp; one index of dp lists at most 3 tiles of one holder, and each index lists exactly 3 from some holder. `tile_docs`: never falls along one index's list; every document reads 4 or more tiles. `tile_rows`: lies within the rows of the tile's document; the first listed tile of each document is visible from the document's first row. `doc_ends`: rising along one index; the last of each index is 128; document j begins where document j - 1 ends, the first at row 0.
All inputs are finite; a program needn't handle non-finite values.
Results may differ from the reference program's by a relative error of at most 0.013.
Values may be sent and summed in bfloat16 or wider, within the bound.
No kernel may reach another device: no remote copies, remote signals or barrier semaphores. Data moves between devices by JAX's collectives and lax.ppermute only.
A program may use at most 64 MiB of HBM per device.

```python
import math
import jax
import jax.numpy as jnp
from jax import lax

H = 64
KVH = 8
HD = 128
TOK_DEV = 128
TILE = 16
SLOTS = 128
DOCS = 8
TEXT = 8192
NTILES = 8192
N_DP = 64


def layout(key):
    per_owner = SLOTS // N_DP
    sigma = jax.random.permutation(jax.random.fold_in(key, 11), N_DP).astype(jnp.int32)
    offset = jax.random.randint(jax.random.fold_in(key, 12), (), 1, N_DP)
    tau_owner = sigma[(jnp.arange(N_DP) + offset) % N_DP]
    base = jnp.broadcast_to((jnp.arange(SLOTS, dtype=jnp.int32) // per_owner)[None, :], (N_DP, SLOTS))
    base = base.at[jnp.arange(N_DP), tau_owner * per_owner].set(sigma)
    row_keys = jax.random.split(jax.random.fold_in(key, 13), N_DP)
    shuffles = jax.vmap(lambda key_one: jax.random.permutation(key_one, SLOTS))(row_keys)
    owners = jnp.take_along_axis(base, shuffles, axis=1)
    onehot = (owners[:, :, None] == jnp.arange(N_DP)[None, None, :]).astype(jnp.int32)
    counts = jnp.sum(onehot, axis=1)
    before = jnp.cumsum(counts, axis=0) - counts
    within = jnp.cumsum(onehot, axis=1) - onehot
    ranking = jnp.sum(onehot * (before[:, None, :] + within), axis=2)
    owner_keys = jax.random.split(jax.random.fold_in(key, 14), N_DP)
    owner_perm = jax.vmap(lambda key_one: jax.random.permutation(key_one, SLOTS))(owner_keys).astype(jnp.int32)
    tiles = owners * SLOTS + owner_perm[owners, ranking]
    spare = SLOTS - 4 * DOCS
    unit_docs = jax.random.randint(jax.random.fold_in(key, 15), (N_DP, spare), 0, DOCS)
    extra = jnp.sum((unit_docs[:, :, None] == jnp.arange(DOCS)[None, None, :]).astype(jnp.int32), axis=1)
    tile_count = 4 + extra
    tile_end = jnp.cumsum(tile_count, axis=1)
    tile_begin = tile_end - tile_count
    slot_index = jnp.arange(SLOTS, dtype=jnp.int32)
    docs_of = jnp.sum((slot_index[None, :, None] >= tile_end[:, None, :]).astype(jnp.int32), axis=2)
    cut_keys = jax.random.split(jax.random.fold_in(key, 16), N_DP)
    cuts = jax.vmap(lambda key_one: jnp.sort(jax.random.permutation(key_one, TOK_DEV - 1)[:DOCS - 1] + 1))(cut_keys).astype(jnp.int32)
    doc_end = jnp.concatenate([cuts, jnp.full((N_DP, 1), TOK_DEV, jnp.int32)], axis=1)
    doc_begin = jnp.concatenate([jnp.zeros((N_DP, 1), jnp.int32), cuts], axis=1)
    begin_of = jnp.take_along_axis(doc_begin, docs_of, axis=1)
    end_of = jnp.take_along_axis(doc_end, docs_of, axis=1)
    first = jnp.take_along_axis(tile_begin, docs_of, axis=1) == slot_index[None, :]
    jitter = jax.random.randint(jax.random.fold_in(key, 17), (N_DP, SLOTS), 0, 1 << 20)
    rows = jnp.where(first, begin_of, begin_of + jitter % (end_of - begin_of))
    return (tiles.reshape(-1).astype(jnp.int32), docs_of.reshape(-1).astype(jnp.int32), rows.reshape(-1).astype(jnp.int32), doc_end.reshape(-1).astype(jnp.int32))


def draw_req_tiles(key, part):
    shared = layout(key)
    return shared[0]


def draw_tile_docs(key, part):
    shared = layout(key)
    return shared[1]


def draw_tile_rows(key, part):
    shared = layout(key)
    return shared[2]


def draw_doc_ends(key, part):
    shared = layout(key)
    return shared[3]


def draw_queries(key, part):
    key = jax.random.fold_in(key, 2)
    values = jnp.clip(jax.random.normal(key, (TEXT, H * HD), jnp.float32), -4.0, 4.0)
    return values.astype(jnp.bfloat16)


def draw_keys_in(key, part):
    key = jax.random.fold_in(key, 6)
    values = jnp.clip(jax.random.normal(key, (NTILES, TILE, KVH * HD), jnp.float32), -4.0, 4.0)
    return values.astype(jnp.bfloat16)


def shard_levels(key, dims, shards, smallest, top_value):
    def one(position, blocks):
        steps = jax.random.uniform(jax.random.fold_in(jax.random.fold_in(key, 6), position), (blocks,), jnp.float32, smallest / len(shards), top_value / len(shards))
        return jnp.repeat(jnp.exp(steps), dims[position] // blocks).reshape((-1,) + (1,) * (len(dims) - position - 1))

    factor_of = one(*shards[0])
    for cut in shards[1:]:
        factor_of = factor_of * one(*cut)
    return factor_of


def bell_draw(stream_key, extent, width, bound, cuts=(), kind=jnp.bfloat16):
    factor_of = shard_levels(stream_key, extent, cuts, -0.22, 0.18) if cuts else 1.0
    result = jax.random.normal(stream_key, extent, jnp.float32) * width * factor_of
    return jnp.minimum(jnp.maximum(result, -bound), bound).astype(kind)


def setup_inputs(seed: int = 0) -> dict:
    splits = jax.random.split(jax.random.key(seed), 9)
    return {
        "queries": draw_queries(jax.random.fold_in(splits[8], 71), 0),
        "keys_in": draw_keys_in(jax.random.fold_in(splits[8], 71), 0),
        "values_in": bell_draw(splits[2], (NTILES, TILE, KVH * HD), 1.0, 4.0, ((0, 64), (1, 8))),
        "dout": bell_draw(splits[3], (TEXT, H * HD), 1.0, 4.0, ((0, 64), (1, 8))),
        "req_tiles": draw_req_tiles(jax.random.fold_in(splits[8], 71), 0),
        "tile_docs": draw_tile_docs(jax.random.fold_in(splits[8], 71), 0),
        "tile_rows": draw_tile_rows(jax.random.fold_in(splits[8], 71), 0),
        "doc_ends": draw_doc_ends(jax.random.fold_in(splits[8], 71), 0),
    }


def attend_group(query_group, key_rows, value_rows, dout_group, visible):
    scale = 1.0 / math.sqrt(HD)
    scores = jnp.einsum('rgd,kd->rgk', query_group.astype(jnp.float32), key_rows.astype(jnp.float32)) * scale
    scores = jnp.where(visible[:, None, :], scores, -1e+30)
    top = lax.optimization_barrier(jnp.max(scores, axis=-1, keepdims=True))
    expo = jnp.exp(scores - top)
    probs = expo / lax.optimization_barrier(jnp.sum(expo, axis=-1, keepdims=True))
    probs_low = probs.astype(jnp.bfloat16)
    output = jnp.einsum('rgk,kd->rgd', probs_low.astype(jnp.float32), value_rows.astype(jnp.float32))
    delta = lax.optimization_barrier(jnp.sum(dout_group.astype(jnp.float32) * output, axis=-1, keepdims=True))
    dprobs = jnp.einsum('rgd,kd->rgk', dout_group.astype(jnp.float32), value_rows.astype(jnp.float32))
    dscores = (probs * (dprobs - delta)).astype(jnp.bfloat16)
    grad_q = jnp.einsum('rgk,kd->rgd', dscores.astype(jnp.float32), key_rows.astype(jnp.float32)) * scale
    grad_k = jnp.einsum('rgk,rgd->kd', dscores.astype(jnp.float32), query_group.astype(jnp.float32)) * scale
    grad_v = jnp.einsum('rgk,rgd->kd', probs_low.astype(jnp.float32), dout_group.astype(jnp.float32))
    return (grad_q, grad_k, grad_v)

def reference(queries, keys_in, values_in, dout, req_tiles, tile_docs, tile_rows, doc_ends):
    group = H // KVH

    def one_index(index):
        slot_start = (index * SLOTS).astype(jnp.int32)
        row_start = (index * TOK_DEV).astype(jnp.int32)
        doc_start = (index * DOCS).astype(jnp.int32)
        tile_ids = lax.dynamic_slice_in_dim(req_tiles, slot_start, SLOTS)
        docs_here = lax.dynamic_slice_in_dim(tile_docs, slot_start, SLOTS)
        rows_here = lax.dynamic_slice_in_dim(tile_rows, slot_start, SLOTS)
        ends_here = lax.dynamic_slice_in_dim(doc_ends, doc_start, DOCS)
        query_rows = lax.dynamic_slice_in_dim(queries, row_start, TOK_DEV, 0)
        dout_rows = lax.dynamic_slice_in_dim(dout, row_start, TOK_DEV, 0)
        key_rows = keys_in[tile_ids].reshape(SLOTS * TILE, KVH * HD)
        value_rows = values_in[tile_ids].reshape(SLOTS * TILE, KVH * HD)
        slot_ends = ends_here[docs_here]
        text_row = jnp.arange(TOK_DEV, dtype=jnp.int32)[:, None]
        seen = (text_row >= rows_here[None, :]) & (text_row < slot_ends[None, :])
        visible = jnp.repeat(seen, TILE, axis=1)
        grads_q, grads_k, grads_v = ([], [], [])
        for kv_head in range(KVH):
            cols = slice(kv_head * group * HD, (kv_head + 1) * group * HD)
            query_group = query_rows[:, cols].reshape(TOK_DEV, group, HD)
            dout_group = dout_rows[:, cols].reshape(TOK_DEV, group, HD)
            kv_cols = slice(kv_head * HD, (kv_head + 1) * HD)
            grad_q, grad_k, grad_v = attend_group(query_group, key_rows[:, kv_cols], value_rows[:, kv_cols], dout_group, visible)
            grads_q.append(grad_q.reshape(TOK_DEV, group * HD).astype(jnp.bfloat16))
            grads_k.append(grad_k.astype(jnp.bfloat16))
            grads_v.append(grad_v.astype(jnp.bfloat16))
        grad_q_all = jnp.concatenate(grads_q, axis=1)
        grad_k_all = jnp.concatenate(grads_k, axis=1).reshape(SLOTS, TILE, KVH * HD)
        grad_v_all = jnp.concatenate(grads_v, axis=1).reshape(SLOTS, TILE, KVH * HD)
        return (grad_q_all, grad_k_all, grad_v_all)
    grad_q_all, grad_k_all, grad_v_all = lax.map(one_index, jnp.arange(N_DP, dtype=jnp.int32))
    grad_queries = grad_q_all.reshape(TEXT, H * HD)
    grad_keys = jnp.zeros((NTILES, TILE, KVH * HD), jnp.bfloat16).at[req_tiles].set(grad_k_all.reshape(NTILES, TILE, KVH * HD))
    grad_values = jnp.zeros((NTILES, TILE, KVH * HD), jnp.bfloat16).at[req_tiles].set(grad_v_all.reshape(NTILES, TILE, KVH * HD))
    return (grad_queries, grad_keys, grad_values)
```

```python
import math

import jax
import jax.numpy as jnp
from jax import lax
from jax.experimental import pallas as pl
from jax.experimental.pallas import tpu as pltpu
from jax.sharding import PartitionSpec as P

HD = 128
BF16 = jnp.bfloat16
F32 = jnp.float32
HIDDEN = -1e30
VMEM_LIMIT = 48 * 1024 * 1024


def pick_tiles(wanted_ref, keys_ref, values_ref, send_ref):
    readers, _, capacity = wanted_ref.shape
    heads = keys_ref.shape[2] // HD

    def one_reader(reader, carry):
        for rank in range(capacity):
            tile = jnp.maximum(wanted_ref[reader, 0, rank], 0)
            for head in range(heads):
                cols = slice(head * HD, (head + 1) * HD)
                send_ref[reader * heads + head, rank] = keys_ref[tile, :, cols]
                send_ref[reader * heads + head, capacity + rank] = values_ref[tile, :, cols]
        return carry

    lax.fori_loop(0, readers, one_reader, 0)


def place_tiles(wanted_ref, home_ref, grad_keys_ref, grad_values_ref):
    readers, _, capacity = wanted_ref.shape
    heads = grad_keys_ref.shape[2] // HD

    def one_reader(reader, carry):
        for rank in range(capacity):
            tile = wanted_ref[reader, 0, rank]

            @pl.when(tile >= 0)
            def _():
                for head in range(heads):
                    cols = slice(head * HD, (head + 1) * HD)
                    grad_keys_ref[tile, :, cols] = home_ref[reader * heads + head, rank]
                    grad_values_ref[tile, :, cols] = home_ref[
                        reader * heads + head, capacity + rank
                    ]

        return carry

    lax.fori_loop(0, readers, one_reader, 0)


def attend_backward(
    holder_ref,
    rank_ref,
    bias_ref,
    recv_ref,
    queries_ref,
    dout_ref,
    back_ref,
    grad_queries_ref,
    key_scr,
    value_scr,
    bias_scr,
    query_scr,
    dout_scr,
    score_scr,
    dprob_scr,
    low_scr,
    dscore_scr,
):
    scale = 1.0 / math.sqrt(HD)
    slots, rows = bias_ref.shape
    capacity = recv_ref.shape[1] // 2
    tile_len = key_scr.shape[0] // slots
    pieces = tile_len // recv_ref.shape[2]
    group = queries_ref.shape[1] // HD
    key_count = slots * tile_len
    chunk = 256
    chunks = key_count // chunk
    pair = 2 * rows
    contract_last = (((1,), (1,)), ((), ()))
    contract_first = (((0,), (0,)), ((), ()))

    def gather_slot(slot, carry):
        source = pl.ds(holder_ref[slot] * pieces, pieces)
        rank = rank_ref[slot]
        target = pl.ds(pl.multiple_of(slot * tile_len, tile_len), tile_len)
        key_scr[target, :] = recv_ref[source, rank].reshape(tile_len, HD)
        value_scr[target, :] = recv_ref[source, capacity + rank].reshape(tile_len, HD)
        bias_scr[target, :] = jnp.broadcast_to(bias_ref[pl.ds(slot, 1), :], (tile_len, rows))
        return carry

    lax.fori_loop(0, slots, gather_slot, 0)

    for head in range(group):
        cols = slice(head * HD, (head + 1) * HD)
        query_scr[head * rows : (head + 1) * rows, :] = queries_ref[:, cols]
        dout_scr[head * rows : (head + 1) * rows, :] = dout_ref[:, cols]

    def one_pair(index, carry):
        start = pl.multiple_of(index * pair, pair)
        query_pair = query_scr[pl.ds(start, pair), :]
        dout_pair = dout_scr[pl.ds(start, pair), :]

        def keys_of(step):
            return pl.ds(pl.multiple_of(step * chunk, chunk), chunk)

        def score_step(step, top):
            where = keys_of(step)
            bias = bias_scr[where, :]
            score = (
                lax.dot_general(
                    key_scr[where, :], query_pair, contract_last, preferred_element_type=F32
                )
                * scale
            )
            score = score + jnp.concatenate([bias, bias], axis=1)
            score_scr[where, :] = score
            return jnp.maximum(top, jnp.max(score, axis=0, keepdims=True))

        top = lax.fori_loop(0, chunks, score_step, jnp.full((1, pair), HIDDEN, F32))

        def exp_step(step, total):
            where = keys_of(step)
            expo = jnp.exp(score_scr[where, :] - top)
            score_scr[where, :] = expo
            return total + jnp.sum(expo, axis=0, keepdims=True)

        total = lax.fori_loop(0, chunks, exp_step, jnp.zeros((1, pair), F32))
        inverse = 1.0 / total

        def prob_step(step, delta):
            where = keys_of(step)
            prob = score_scr[where, :] * inverse
            low = prob.astype(BF16)
            dprob = lax.dot_general(
                value_scr[where, :], dout_pair, contract_last, preferred_element_type=F32
            )
            score_scr[where, :] = prob
            dprob_scr[where, :] = dprob
            low_scr[where, pl.ds(start, pair)] = low
            return delta + jnp.sum(low.astype(F32) * dprob, axis=0, keepdims=True)

        delta = lax.fori_loop(0, chunks, prob_step, jnp.zeros((1, pair), F32))

        def dscore_step(step, grad):
            where = keys_of(step)
            dscore = (score_scr[where, :] * (dprob_scr[where, :] - delta)).astype(BF16)
            dscore_scr[where, pl.ds(start, pair)] = dscore
            return grad + lax.dot_general(
                dscore, key_scr[where, :], contract_first, preferred_element_type=F32
            )

        grad = lax.fori_loop(0, chunks, dscore_step, jnp.zeros((pair, HD), F32)) * scale
        query_scr_out = grad.astype(BF16)
        grad_queries_ref[:, pl.ds(pl.multiple_of(index * 2 * HD, 2 * HD), HD)] = query_scr_out[
            :rows
        ]
        grad_queries_ref[:, pl.ds(pl.multiple_of(index * 2 * HD + HD, HD), HD)] = query_scr_out[
            rows:
        ]
        return carry

    lax.fori_loop(0, group // 2, one_pair, 0)

    def key_step(step, carry):
        where = pl.ds(pl.multiple_of(step * chunk, chunk), chunk)
        grad_value = lax.dot_general(
            low_scr[where, :], dout_scr[...], (((1,), (0,)), ((), ())), preferred_element_type=F32
        ).astype(BF16)
        grad_key = (
            lax.dot_general(
                dscore_scr[where, :],
                query_scr[...],
                (((1,), (0,)), ((), ())),
                preferred_element_type=F32,
            )
            * scale
        ).astype(BF16)
        per_chunk = chunk // tile_len
        for k in range(per_chunk):
            slot = step * per_chunk + k
            source = pl.ds(holder_ref[slot] * pieces, pieces)
            rank = rank_ref[slot]
            part = slice(k * tile_len, (k + 1) * tile_len)
            back_ref[source, rank] = grad_key[part].reshape(pieces, tile_len // pieces, HD)
            back_ref[source, capacity + rank] = grad_value[part].reshape(
                pieces, tile_len // pieces, HD
            )
        return carry

    lax.fori_loop(0, chunks, key_step, 0)


def per_device(queries, keys_in, values_in, dout, req_tiles, tile_docs, tile_rows, doc_ends):
    dp_count = lax.axis_size("dp")
    heads = lax.axis_size("tensor")
    slots = req_tiles.shape[0]
    capacity = slots // dp_count + 1
    row_part = keys_in.shape[1]
    rows = queries.shape[0]
    smem = pl.BlockSpec(memory_space=pltpu.SMEM)
    vmem = pl.BlockSpec(memory_space=pltpu.VMEM)
    params = pltpu.CompilerParams(vmem_limit_bytes=VMEM_LIMIT)

    holder = req_tiles // slots
    slot_index = jnp.arange(slots, dtype=jnp.int32)
    same_before = (holder[:, None] == holder[None, :]) & (slot_index[None, :] < slot_index[:, None])
    rank = jnp.sum(same_before.astype(jnp.int32), axis=1)
    place = holder * HD + rank
    lanes = jnp.arange(dp_count * HD, dtype=jnp.int32).reshape(dp_count, HD)
    asked = jnp.sum(
        jnp.where(place[None, None, :] == lanes[:, :capacity, None], (req_tiles % slots + 1)[None, None, :], 0),
        axis=-1,
    )
    asked = jnp.pad(asked - 1, ((0, 0), (0, HD - capacity)))[:, None, :]
    wanted = lax.all_to_all(asked, "dp", split_axis=0, concat_axis=0, tiled=True)[:, :, :capacity]

    send = pl.pallas_call(
        pick_tiles,
        out_shape=jax.ShapeDtypeStruct((dp_count * heads, 2 * capacity, row_part, HD), BF16),
        in_specs=[smem, vmem, vmem],
        out_specs=vmem,
        compiler_params=params,
        name="pick_tiles",
    )(wanted, keys_in, values_in)
    recv = lax.all_to_all(send, ("dp", "tensor"), split_axis=0, concat_axis=0, tiled=True)

    doc_count = doc_ends.shape[0]
    slot_ends = jnp.sum(
        jnp.where(
            tile_docs[:, None] == jnp.arange(doc_count, dtype=jnp.int32)[None, :],
            doc_ends[None, :],
            0,
        ),
        axis=1,
    )
    text_row = jnp.arange(rows, dtype=jnp.int32)[None, :]
    seen = (text_row >= tile_rows[:, None]) & (text_row < slot_ends[:, None])
    bias = jnp.where(seen, 0.0, HIDDEN).astype(F32)

    key_count = slots * row_part * heads
    group = queries.shape[1] // HD
    back, grad_queries = pl.pallas_call(
        attend_backward,
        out_shape=(
            jax.ShapeDtypeStruct(recv.shape, BF16),
            jax.ShapeDtypeStruct(queries.shape, BF16),
        ),
        in_specs=[smem, smem, vmem, vmem, vmem, vmem],
        out_specs=(vmem, vmem),
        scratch_shapes=[
            pltpu.VMEM((key_count, HD), BF16),
            pltpu.VMEM((key_count, HD), BF16),
            pltpu.VMEM((key_count, rows), F32),
            pltpu.VMEM((group * rows, HD), BF16),
            pltpu.VMEM((group * rows, HD), BF16),
            pltpu.VMEM((key_count, 2 * rows), F32),
            pltpu.VMEM((key_count, 2 * rows), F32),
            pltpu.VMEM((key_count, group * rows), BF16),
            pltpu.VMEM((key_count, group * rows), BF16),
        ],
        compiler_params=params,
        name="attend_backward",
    )(holder, rank, bias, recv, queries, dout)

    home = lax.all_to_all(back, ("dp", "tensor"), split_axis=0, concat_axis=0, tiled=True)
    grad_keys, grad_values = pl.pallas_call(
        place_tiles,
        out_shape=(
            jax.ShapeDtypeStruct(keys_in.shape, BF16),
            jax.ShapeDtypeStruct(values_in.shape, BF16),
        ),
        in_specs=[smem, vmem],
        out_specs=(vmem, vmem),
        compiler_params=params,
        name="place_tiles",
    )(wanted, home)
    return (grad_queries, grad_keys, grad_values)


def solution(mesh):
    return jax.shard_map(
        per_device,
        mesh=mesh,
        in_specs=(
            P("dp", "tensor"),
            P("dp", "tensor", None),
            P("dp", "tensor", None),
            P("dp", "tensor"),
            P("dp"),
            P("dp"),
            P("dp"),
            P("dp"),
        ),
        out_specs=(P("dp", "tensor"), P("dp", "tensor", None), P("dp", "tensor", None)),
        check_vma=False,
    )
```

```python
import math

import jax
import jax.numpy as jnp
from jax import lax
from jax.experimental import pallas as pl
from jax.experimental.pallas import tpu as pltpu
from jax.sharding import PartitionSpec as P

HD = 128
TILE = 16
BF16 = jnp.bfloat16
F32 = jnp.float32
HIDDEN = -1e30
CHUNK = 512
BLOCK = 256
VMEM_LIMIT = 48 * 1024 * 1024


def pick_tiles(wanted_ref, keys_ref, values_ref, send_ref):
    readers, _, capacity = wanted_ref.shape
    heads = keys_ref.shape[2] // HD

    def one_reader(reader, carry):
        for rank in range(capacity):
            tile = jnp.maximum(wanted_ref[reader, 0, rank], 0)
            for head in range(heads):
                cols = slice(head * HD, (head + 1) * HD)
                send_ref[reader * heads + head, rank] = keys_ref[tile, :, cols]
                send_ref[reader * heads + head, capacity + rank] = values_ref[tile, :, cols]
        return carry

    lax.fori_loop(0, readers, one_reader, 0)


def place_tiles(wanted_ref, home_ref, grad_keys_ref, grad_values_ref):
    readers, _, capacity = wanted_ref.shape
    heads = grad_keys_ref.shape[2] // HD

    def one_reader(reader, carry):
        for rank in range(capacity):
            tile = wanted_ref[reader, 0, rank]

            @pl.when(tile >= 0)
            def _():
                for head in range(heads):
                    cols = slice(head * HD, (head + 1) * HD)
                    grad_keys_ref[tile, :, cols] = home_ref[reader * heads + head, rank]
                    grad_values_ref[tile, :, cols] = home_ref[
                        reader * heads + head, capacity + rank
                    ]

        return carry

    lax.fori_loop(0, readers, one_reader, 0)


def attend_backward(
    holder_ref,
    rank_ref,
    first_ref,
    last_ref,
    bias_ref,
    recv_ref,
    queries_ref,
    dout_ref,
    back_ref,
    grad_queries_ref,
    key_scr,
    value_scr,
    expo_scr,
    dprob_scr,
    top_scr,
    grad_key_scr,
    grad_value_scr,
):
    scale = 1.0 / math.sqrt(HD)
    slots = bias_ref.shape[0]
    capacity = recv_ref.shape[1] // 2
    tile_len = key_scr.shape[0] // slots
    pieces = tile_len // recv_ref.shape[2]
    chunk, block = expo_scr.shape[1:]
    blocks = queries_ref.shape[0] // block
    contract_last = (((1,), (1,)), ((), ()))
    contract_inner = (((1,), (0,)), ((), ()))
    contract_first = (((0,), (0,)), ((), ()))

    def gather_slot(slot, carry):
        source = pl.ds(holder_ref[slot] * pieces, pieces)
        rank = rank_ref[slot]
        target = pl.ds(pl.multiple_of(slot * tile_len, tile_len), tile_len)
        key_scr[target, :HD] = recv_ref[source, rank].reshape(tile_len, HD)
        key_scr[target, HD:] = jnp.broadcast_to(bias_ref[pl.ds(slot, 1), :], (tile_len, HD)).astype(
            BF16
        )
        value_scr[target, :] = recv_ref[source, capacity + rank].reshape(tile_len, HD)
        return carry

    lax.fori_loop(0, slots, gather_slot, 0, unroll=8)
    grad_key_scr[...] = jnp.zeros_like(grad_key_scr)
    grad_value_scr[...] = jnp.zeros_like(grad_value_scr)

    def one_block(index, carry):
        rows = pl.ds(pl.multiple_of(index * block, block), block)
        first, last = first_ref[index], last_ref[index]

        def keys_of(step):
            return pl.ds(pl.multiple_of(step * chunk, chunk), chunk)

        def forward(step, carry):
            top, total, delta = carry
            where = keys_of(step)
            score = lax.dot_general(
                key_scr[where, :], queries_ref[rows, :], contract_last, preferred_element_type=F32
            )
            dprob = lax.dot_general(
                value_scr[where, :], dout_ref[rows, :], contract_last, preferred_element_type=F32
            )
            new_top = jnp.maximum(top, jnp.max(score, axis=0, keepdims=True))
            shrink = jnp.exp((top - new_top) * scale)
            expo = jnp.exp((score - new_top) * scale)
            expo_scr[step] = expo
            dprob_scr[step] = dprob
            top_scr[pl.ds(step, 1), :] = new_top
            return (
                new_top,
                total * shrink + jnp.sum(expo, axis=0, keepdims=True),
                delta * shrink + jnp.sum(expo * dprob, axis=0, keepdims=True),
            )

        zero = jnp.zeros((1, block), F32)
        top, total, delta = lax.fori_loop(
            first, last, forward, (jnp.full((1, block), 2 * HIDDEN, F32), zero, zero)
        )
        inverse = 1.0 / total
        delta = delta * inverse

        def backward(step, grad_query):
            where = keys_of(step)
            factor = jnp.exp((top_scr[pl.ds(step, 1), :] - top) * scale) * inverse
            prob = expo_scr[step] * factor
            dscore = (prob * (dprob_scr[step] - delta)).astype(BF16)
            grad_value_scr[where, :] += lax.dot_general(
                prob.astype(BF16), dout_ref[rows, :], contract_inner, preferred_element_type=F32
            )
            grad_key_scr[where, :] += lax.dot_general(
                dscore, queries_ref[rows, :HD], contract_inner, preferred_element_type=F32
            )
            return grad_query + lax.dot_general(
                dscore, key_scr[where, :HD], contract_first, preferred_element_type=F32
            )

        grad_query = lax.fori_loop(first, last, backward, jnp.zeros((block, HD), F32))
        grad_queries_ref[rows, :] = (grad_query * scale).astype(BF16)
        return carry

    lax.fori_loop(0, blocks, one_block, 0)

    def return_slot(slot, carry):
        source = pl.ds(holder_ref[slot] * pieces, pieces)
        rank = rank_ref[slot]
        where = pl.ds(pl.multiple_of(slot * tile_len, tile_len), tile_len)
        shape = (pieces, tile_len // pieces, HD)
        back_ref[source, rank] = (grad_key_scr[where, :] * scale).astype(BF16).reshape(shape)
        back_ref[source, capacity + rank] = grad_value_scr[where, :].astype(BF16).reshape(shape)
        return carry

    lax.fori_loop(0, slots, return_slot, 0, unroll=8)


def attention(recv, queries, dout, holder, rank, tile_docs, tile_rows, doc_ends):
    slots, rows = holder.shape[0], queries.shape[0]
    smem = pl.BlockSpec(memory_space=pltpu.SMEM)
    vmem = pl.BlockSpec(memory_space=pltpu.VMEM)
    group = queries.shape[1] // HD
    docs = tile_docs[:, None] == jnp.arange(doc_ends.shape[0], dtype=jnp.int32)[None, :]
    slot_ends = jnp.sum(jnp.where(docs, doc_ends[None, :], 0), axis=1)
    slot_begins = jnp.sum(jnp.where(docs[:, 1:], doc_ends[None, :-1], 0), axis=1)
    text_row = jnp.arange(rows, dtype=jnp.int32)
    seen = (text_row[None, :] >= tile_rows[:, None]) & (text_row[None, :] < slot_ends[:, None])
    bias = jnp.where(seen, 0.0, HIDDEN).astype(F32)
    tile_len = TILE
    chunk_slots = CHUNK // tile_len
    block_begin = jnp.arange(rows * group // BLOCK, dtype=jnp.int32) * (BLOCK // group)
    before = jnp.sum((slot_ends[None, :] <= block_begin[:, None]).astype(jnp.int32), axis=1)
    until = jnp.sum(
        (slot_begins[None, :] < block_begin[:, None] + BLOCK // group).astype(jnp.int32), axis=1
    )
    first = before // chunk_slots
    last = (until + chunk_slots - 1) // chunk_slots

    flat = rows * group
    query_rows = queries.reshape(flat, HD)
    dout_rows = dout.reshape(flat, HD)
    own_row = (jnp.arange(flat, dtype=jnp.int32) // group)[:, None] == text_row[None, :]
    query_rows = jnp.concatenate([query_rows, own_row.astype(BF16)], axis=1)

    key_count = slots * tile_len
    return pl.pallas_call(
        attend_backward,
        out_shape=(
            jax.ShapeDtypeStruct(recv.shape, BF16),
            jax.ShapeDtypeStruct((flat, HD), BF16),
        ),
        in_specs=[smem] * 4 + [vmem] * 4,
        out_specs=(vmem, vmem),
        scratch_shapes=[
            pltpu.VMEM((key_count, 2 * HD), BF16),
            pltpu.VMEM((key_count, HD), BF16),
            pltpu.VMEM((key_count // CHUNK, CHUNK, BLOCK), F32),
            pltpu.VMEM((key_count // CHUNK, CHUNK, BLOCK), F32),
            pltpu.VMEM((key_count // CHUNK, BLOCK), F32),
            pltpu.VMEM((key_count, HD), F32),
            pltpu.VMEM((key_count, HD), F32),
        ],
        compiler_params=pltpu.CompilerParams(vmem_limit_bytes=VMEM_LIMIT),
        name="attend_backward",
    )(holder, rank, first, last, bias, recv, query_rows, dout_rows)


def per_device(queries, keys_in, values_in, dout, req_tiles, tile_docs, tile_rows, doc_ends):
    dp_count = lax.axis_size("dp")
    heads = lax.axis_size("tensor")
    slots = req_tiles.shape[0]
    capacity = slots // dp_count + 1
    row_part = keys_in.shape[1]
    rows = queries.shape[0]
    smem = pl.BlockSpec(memory_space=pltpu.SMEM)
    vmem = pl.BlockSpec(memory_space=pltpu.VMEM)
    params = pltpu.CompilerParams(vmem_limit_bytes=VMEM_LIMIT)

    holder = req_tiles // slots
    slot_index = jnp.arange(slots, dtype=jnp.int32)
    same_before = (holder[:, None] == holder[None, :]) & (slot_index[None, :] < slot_index[:, None])
    rank = jnp.sum(same_before.astype(jnp.int32), axis=1)
    place = holder * HD + rank
    lanes = jnp.arange(dp_count * HD, dtype=jnp.int32).reshape(dp_count, HD)
    asked = jnp.sum(
        jnp.where(place[None, None, :] == lanes[:, :capacity, None], (req_tiles % slots + 1)[None, None, :], 0),
        axis=-1,
    )
    asked = jnp.pad(asked - 1, ((0, 0), (0, HD - capacity)))[:, None, :]
    wanted = lax.all_to_all(asked, "dp", split_axis=0, concat_axis=0, tiled=True)[:, :, :capacity]

    send = pl.pallas_call(
        pick_tiles,
        out_shape=jax.ShapeDtypeStruct((dp_count * heads, 2 * capacity, row_part, HD), BF16),
        in_specs=[smem, vmem, vmem],
        out_specs=vmem,
        compiler_params=params,
        name="pick_tiles",
    )(wanted, keys_in, values_in)
    recv = lax.all_to_all(send, ("dp", "tensor"), split_axis=0, concat_axis=0, tiled=True)

    back, grad_queries = attention(
        recv, queries, dout, holder, rank, tile_docs, tile_rows, doc_ends
    )

    home = lax.all_to_all(back, ("dp", "tensor"), split_axis=0, concat_axis=0, tiled=True)
    grad_keys, grad_values = pl.pallas_call(
        place_tiles,
        out_shape=(
            jax.ShapeDtypeStruct(keys_in.shape, BF16),
            jax.ShapeDtypeStruct(values_in.shape, BF16),
        ),
        in_specs=[smem, vmem],
        out_specs=(vmem, vmem),
        compiler_params=params,
        name="place_tiles",
    )(wanted, home)
    return (grad_queries.reshape(queries.shape), grad_keys, grad_values)


def solution(mesh):
    return jax.shard_map(
        per_device,
        mesh=mesh,
        in_specs=(
            P("dp", "tensor"),
            P("dp", "tensor", None),
            P("dp", "tensor", None),
            P("dp", "tensor"),
            P("dp"),
            P("dp"),
            P("dp"),
            P("dp"),
        ),
        out_specs=(P("dp", "tensor"), P("dp", "tensor", None), P("dp", "tensor", None)),
        check_vma=False,
    )
```

```python
import math

import jax
import jax.numpy as jnp
from jax import lax
from jax.experimental import pallas as pl
from jax.experimental.pallas import tpu as pltpu
from jax.sharding import PartitionSpec as P

HD = 128
TILE = 16
BF16 = jnp.bfloat16
F32 = jnp.float32
HIDDEN = -1e30
CHUNK = 512
BLOCK = 256
PARTS = 4
VMEM_LIMIT = 48 * 1024 * 1024


def pick_tiles(
    wanted_ref, keys_hbm, values_hbm, send_hbm, keys_ref, values_ref, send_ref, in_sem, out_sem
):
    readers, _, capacity = wanted_ref.shape
    heads = keys_ref.shape[2] // HD
    loads = [
        pltpu.make_async_copy(keys_hbm, keys_ref, in_sem.at[0]),
        pltpu.make_async_copy(values_hbm, values_ref, in_sem.at[1]),
    ]
    for load in loads:
        load.start()
    for load in loads:
        load.wait()

    part = readers // PARTS
    stores = []
    for step in range(PARTS):

        def one_reader(offset, carry):
            reader = step * part + offset

            def one_tile(rank):
                tile = jnp.maximum(wanted_ref[reader, 0, rank], 0)
                for head in range(heads):
                    cols = slice(head * HD, (head + 1) * HD)
                    send_ref[reader * heads + head, rank] = keys_ref[tile, :, cols]
                    send_ref[reader * heads + head, capacity + rank] = values_ref[tile, :, cols]

            for rank in range(capacity):
                one_tile(rank)
            return carry

        lax.fori_loop(0, part, one_reader, 0, unroll=4)
        rows = pl.ds(step * part * heads, part * heads)
        stores.append(pltpu.make_async_copy(send_ref.at[rows], send_hbm.at[rows], out_sem.at[step]))
        stores[-1].start()
    for store in stores:
        store.wait()


def place_tiles(
    source_ref, home_ref, grad_keys_hbm, grad_values_hbm, grad_keys_ref, grad_values_ref, out_sem
):
    chunks, lines = home_ref.shape[:2]
    capacity = lines // 2
    heads = grad_keys_ref.shape[2] // HD
    flat_ref = home_ref.reshape(chunks * lines, *home_ref.shape[2:])
    part = grad_keys_ref.shape[0] // PARTS
    stores = []
    for step in range(PARTS):

        def one_tile(offset, carry):
            tile = step * part + offset
            source = source_ref[tile]
            for head in range(heads):
                cols = slice(head * HD, (head + 1) * HD)
                grad_keys_ref[tile, :, cols] = flat_ref[source + lines * head]
                grad_values_ref[tile, :, cols] = flat_ref[source + lines * head + capacity]
            return carry

        lax.fori_loop(0, part, one_tile, 0, unroll=4)
        rows = pl.ds(step * part, part)
        for kind, (ref, hbm) in enumerate(
            ((grad_keys_ref, grad_keys_hbm), (grad_values_ref, grad_values_hbm))
        ):
            stores.append(
                pltpu.make_async_copy(ref.at[rows], hbm.at[rows], out_sem.at[kind, step])
            )
            stores[-1].start()
    for store in stores:
        store.wait()


def attend_backward(
    holder_ref,
    rank_ref,
    slot_ref,
    first_ref,
    steps_ref,
    bias_ref,
    recv_ref,
    queries_ref,
    dout_ref,
    back_hbm,
    grad_queries_ref,
    key_scr,
    value_scr,
    expo_scr,
    dprob_scr,
    top_scr,
    grad_key_scr,
    grad_value_scr,
    back_ref,
    out_sem,
):
    scale = 1.0 / math.sqrt(HD)
    rate = scale * math.log2(math.e)
    slots = bias_ref.shape[0]
    capacity = recv_ref.shape[1] // 2
    tile_len = TILE
    pieces = tile_len // recv_ref.shape[2]
    chunk, block = expo_scr.shape[1:]
    blocks = queries_ref.shape[0] // block
    key_count = slots * tile_len
    tail = pl.ds(key_count, key_scr.shape[0] - key_count)
    contract_last = (((1,), (1,)), ((), ()))
    contract_inner = (((1,), (0,)), ((), ()))
    contract_first = (((0,), (0,)), ((), ()))

    def gather_slot(slot, carry):
        source = pl.ds(holder_ref[slot] * pieces, pieces)
        rank = rank_ref[slot]
        target = pl.ds(pl.multiple_of(slot * tile_len, tile_len), tile_len)
        key_scr[target, :HD] = recv_ref[source, rank].reshape(tile_len, HD)
        key_scr[target, HD:] = jnp.broadcast_to(bias_ref[pl.ds(slot, 1), :], (tile_len, HD)).astype(
            BF16
        )
        value_scr[target, :] = recv_ref[source, capacity + rank].reshape(tile_len, HD)
        return carry

    lax.fori_loop(0, slots, gather_slot, 0, unroll=8)
    key_scr[tail, :HD] = jnp.zeros((tail.size, HD), BF16)
    key_scr[tail, HD:] = jnp.full((tail.size, HD), HIDDEN, BF16)
    value_scr[tail, :] = jnp.zeros((tail.size, HD), BF16)
    grad_key_scr[...] = jnp.zeros_like(grad_key_scr)
    grad_value_scr[...] = jnp.zeros_like(grad_value_scr)

    def one_block(index, carry):
        rows = pl.ds(pl.multiple_of(index * block, block), block)
        first, steps = first_ref[index], steps_ref[index]

        def keys_of(step):
            return pl.ds(pl.multiple_of(first * tile_len + step * chunk, tile_len), chunk)

        def forward(step, carry):
            top, total, delta = carry
            where = keys_of(step)
            score = lax.dot_general(
                key_scr[where, :], queries_ref[rows, :], contract_last, preferred_element_type=F32
            )
            dprob = lax.dot_general(
                value_scr[where, :], dout_ref[rows, :], contract_last, preferred_element_type=F32
            )
            new_top = jnp.maximum(top, jnp.max(score, axis=0, keepdims=True))
            shrink = jnp.exp2((top - new_top) * rate)
            expo = jnp.exp2((score - new_top) * rate)
            expo_scr[step] = expo
            dprob_scr[step] = dprob
            top_scr[pl.ds(step, 1), :] = new_top
            return (
                new_top,
                total * shrink + jnp.sum(expo, axis=0, keepdims=True),
                delta * shrink + jnp.sum(expo * dprob, axis=0, keepdims=True),
            )

        zero = jnp.zeros((1, block), F32)
        top, total, delta = lax.fori_loop(
            0, steps, forward, (jnp.full((1, block), 2 * HIDDEN, F32), zero, zero)
        )
        inverse = 1.0 / total
        delta = delta * inverse

        def backward(step, grad_query):
            where = keys_of(step)
            factor = jnp.exp2((top_scr[pl.ds(step, 1), :] - top) * rate) * inverse
            prob = expo_scr[step] * factor
            dscore = (prob * (dprob_scr[step] - delta)).astype(BF16)
            grad_value_scr[where, :] += lax.dot_general(
                prob.astype(BF16), dout_ref[rows, :], contract_inner, preferred_element_type=F32
            )
            grad_key_scr[where, :] += lax.dot_general(
                dscore, queries_ref[rows, :HD], contract_inner, preferred_element_type=F32
            )
            return grad_query + lax.dot_general(
                dscore, key_scr[where, :HD], contract_first, preferred_element_type=F32
            )

        grad_query = lax.fori_loop(0, steps, backward, jnp.zeros((block, HD), F32))
        grad_queries_ref[rows, :] = (grad_query * scale).astype(BF16)
        return carry

    lax.fori_loop(0, blocks, one_block, 0)

    part = slot_ref.shape[0] // PARTS
    stores = []
    for step in range(PARTS):

        def return_tiles(offset, carry):
            holder = step * part + offset

            def one_tile(rank):
                slot = jnp.maximum(slot_ref[holder, rank], 0)
                where = pl.ds(pl.multiple_of(slot * tile_len, tile_len), tile_len)
                chunks = pl.ds(holder * pieces, pieces)
                shape = (pieces, tile_len // pieces, HD)
                grad_key = (grad_key_scr[where, :] * scale).astype(BF16)
                back_ref[chunks, rank] = grad_key.reshape(shape)
                grad_value = grad_value_scr[where, :].astype(BF16)
                back_ref[chunks, capacity + rank] = grad_value.reshape(shape)

            for rank in range(capacity):
                one_tile(rank)
            return carry

        lax.fori_loop(0, part, return_tiles, 0, unroll=4)
        chunks = pl.ds(step * part * pieces, part * pieces)
        stores.append(
            pltpu.make_async_copy(back_ref.at[chunks], back_hbm.at[chunks], out_sem.at[step])
        )
        stores[-1].start()
    for store in stores:
        store.wait()


def attention(recv, queries, dout, holder, rank, slot_of, tile_docs, tile_rows, doc_ends):
    slots, rows = holder.shape[0], queries.shape[0]
    smem = pl.BlockSpec(memory_space=pltpu.SMEM)
    vmem = pl.BlockSpec(memory_space=pltpu.VMEM)
    group = queries.shape[1] // HD
    docs = tile_docs[:, None] == jnp.arange(doc_ends.shape[0], dtype=jnp.int32)[None, :]
    slot_ends = jnp.sum(jnp.where(docs, doc_ends[None, :], 0), axis=1)
    slot_begins = jnp.sum(jnp.where(docs[:, 1:], doc_ends[None, :-1], 0), axis=1)
    text_row = jnp.arange(rows, dtype=jnp.int32)
    seen = (text_row[None, :] >= tile_rows[:, None]) & (text_row[None, :] < slot_ends[:, None])
    bias = jnp.where(seen, 0.0, HIDDEN).astype(F32)
    tile_len = TILE
    chunk_slots = CHUNK // tile_len
    block_begin = jnp.arange(rows * group // BLOCK, dtype=jnp.int32) * (BLOCK // group)
    first = jnp.sum((slot_ends[None, :] <= block_begin[:, None]).astype(jnp.int32), axis=1)
    until = jnp.sum(
        (slot_begins[None, :] < block_begin[:, None] + BLOCK // group).astype(jnp.int32), axis=1
    )
    steps = (until - first + chunk_slots - 1) // chunk_slots

    flat = rows * group
    query_rows = queries.reshape(flat, HD)
    dout_rows = dout.reshape(flat, HD)
    own_row = (jnp.arange(flat, dtype=jnp.int32) // group)[:, None] == text_row[None, :]
    query_rows = jnp.concatenate([query_rows, own_row.astype(BF16)], axis=1)

    key_count = slots * tile_len
    return pl.pallas_call(
        attend_backward,
        out_shape=(
            jax.ShapeDtypeStruct(recv.shape, BF16),
            jax.ShapeDtypeStruct((flat, HD), BF16),
        ),
        in_specs=[smem] * 5 + [vmem] * 4,
        out_specs=(pl.BlockSpec(memory_space=pl.ANY), vmem),
        scratch_shapes=[
            pltpu.VMEM((key_count + CHUNK, 2 * HD), BF16),
            pltpu.VMEM((key_count + CHUNK, HD), BF16),
            pltpu.VMEM((key_count // CHUNK, CHUNK, BLOCK), F32),
            pltpu.VMEM((key_count // CHUNK, CHUNK, BLOCK), F32),
            pltpu.VMEM((key_count // CHUNK, BLOCK), F32),
            pltpu.VMEM((key_count + CHUNK, HD), F32),
            pltpu.VMEM((key_count + CHUNK, HD), F32),
            pltpu.VMEM(recv.shape, BF16),
            pltpu.SemaphoreType.DMA((PARTS,)),
        ],
        compiler_params=pltpu.CompilerParams(vmem_limit_bytes=VMEM_LIMIT),
        name="attend_backward",
    )(holder, rank, slot_of, first, steps, bias, recv, query_rows, dout_rows)


def per_device(queries, keys_in, values_in, dout, req_tiles, tile_docs, tile_rows, doc_ends):
    dp_count = lax.axis_size("dp")
    heads = lax.axis_size("tensor")
    slots = req_tiles.shape[0]
    capacity = slots // dp_count + 1
    row_part = keys_in.shape[1]
    rows = queries.shape[0]
    smem = pl.BlockSpec(memory_space=pltpu.SMEM)
    vmem = pl.BlockSpec(memory_space=pltpu.VMEM)
    hbm = pl.BlockSpec(memory_space=pl.ANY)
    params = pltpu.CompilerParams(vmem_limit_bytes=VMEM_LIMIT)

    holder = req_tiles // slots
    slot_index = jnp.arange(slots, dtype=jnp.int32)
    same_before = (holder[:, None] == holder[None, :]) & (slot_index[None, :] < slot_index[:, None])
    rank = jnp.sum(same_before.astype(jnp.int32), axis=1)
    places = jnp.arange(dp_count, dtype=jnp.int32)[:, None, None]
    ranks = jnp.arange(capacity, dtype=jnp.int32)[None, :, None]
    there = (holder[None, None, :] == places) & (rank[None, None, :] == ranks)
    asked = jnp.sum(jnp.where(there, (req_tiles % slots + 1)[None, None, :], 0), axis=-1) - 1
    slot_of = jnp.sum(jnp.where(there, (slot_index + 1)[None, None, :], 0), axis=-1) - 1
    asked = jnp.pad(asked, ((0, 0), (0, HD - capacity)))[:, None, :]
    wanted = lax.all_to_all(asked, "dp", split_axis=0, concat_axis=0, tiled=True)[:, :, :capacity]

    send = pl.pallas_call(
        pick_tiles,
        out_shape=jax.ShapeDtypeStruct((dp_count * heads, 2 * capacity, row_part, HD), BF16),
        in_specs=[smem, hbm, hbm],
        out_specs=hbm,
        scratch_shapes=[
            pltpu.VMEM(keys_in.shape, BF16),
            pltpu.VMEM(values_in.shape, BF16),
            pltpu.VMEM((dp_count * heads, 2 * capacity, row_part, HD), BF16),
            pltpu.SemaphoreType.DMA((2,)),
            pltpu.SemaphoreType.DMA((PARTS,)),
        ],
        compiler_params=params,
        name="pick_tiles",
    )(wanted, keys_in, values_in)
    recv = lax.all_to_all(send, ("dp", "tensor"), split_axis=0, concat_axis=0, tiled=True)

    back, grad_queries = attention(
        recv, queries, dout, holder, rank, slot_of, tile_docs, tile_rows, doc_ends
    )

    home = lax.all_to_all(back, ("dp", "tensor"), split_axis=0, concat_axis=0, tiled=True)
    tile_index = jnp.arange(slots, dtype=jnp.int32)[:, None, None]
    lines = jnp.arange(dp_count, dtype=jnp.int32)[:, None] * (heads * 2 * capacity) + ranks[:, :, 0]
    source = jnp.sum(jnp.where(wanted[:, 0][None] == tile_index, lines[None], 0), axis=(1, 2))
    grad_keys, grad_values = pl.pallas_call(
        place_tiles,
        out_shape=(
            jax.ShapeDtypeStruct(keys_in.shape, BF16),
            jax.ShapeDtypeStruct(values_in.shape, BF16),
        ),
        in_specs=[smem, vmem],
        out_specs=(hbm, hbm),
        scratch_shapes=[
            pltpu.VMEM(keys_in.shape, BF16),
            pltpu.VMEM(values_in.shape, BF16),
            pltpu.SemaphoreType.DMA((2, PARTS)),
        ],
        compiler_params=params,
        name="place_tiles",
    )(source, home)
    return (grad_queries.reshape(queries.shape), grad_keys, grad_values)


def solution(mesh):
    return jax.shard_map(
        per_device,
        mesh=mesh,
        in_specs=(
            P("dp", "tensor"),
            P("dp", "tensor", None),
            P("dp", "tensor", None),
            P("dp", "tensor"),
            P("dp"),
            P("dp"),
            P("dp"),
            P("dp"),
        ),
        out_specs=(P("dp", "tensor"), P("dp", "tensor", None), P("dp", "tensor", None)),
        check_vma=False,
    )
```

```python
import math

import jax
import jax.numpy as jnp
from jax import lax
from jax.experimental import pallas as pl
from jax.experimental.pallas import tpu as pltpu
from jax.sharding import PartitionSpec as P

HD = 128
TILE = 16
BF16 = jnp.bfloat16
F32 = jnp.float32
HIDDEN = -1e30
CHUNK = 512
BLOCK = 256
PARTS = 4
VMEM_LIMIT = 48 * 1024 * 1024


def pick_tiles(
    wanted_ref, keys_hbm, values_hbm, send_hbm, keys_ref, values_ref, send_ref, in_sem, out_sem
):
    readers, _, capacity = wanted_ref.shape
    heads = keys_ref.shape[2] // HD
    loads = [
        pltpu.make_async_copy(keys_hbm, keys_ref, in_sem.at[0]),
        pltpu.make_async_copy(values_hbm, values_ref, in_sem.at[1]),
    ]
    for load in loads:
        load.start()
    for load in loads:
        load.wait()

    part = readers // PARTS
    stores = []
    for step in range(PARTS):

        def one_reader(offset, carry):
            reader = step * part + offset

            def one_tile(rank):
                tile = jnp.maximum(wanted_ref[reader, 0, rank], 0)
                for head in range(heads):
                    cols = slice(head * HD, (head + 1) * HD)
                    send_ref[reader * heads + head, rank] = keys_ref[tile, :, cols]
                    send_ref[reader * heads + head, capacity + rank] = values_ref[tile, :, cols]

            for rank in range(capacity):
                one_tile(rank)
            return carry

        lax.fori_loop(0, part, one_reader, 0, unroll=4)
        rows = pl.ds(step * part * heads, part * heads)
        stores.append(pltpu.make_async_copy(send_ref.at[rows], send_hbm.at[rows], out_sem.at[step]))
        stores[-1].start()
    for store in stores:
        store.wait()


def place_tiles(
    source_ref, home_ref, grad_keys_hbm, grad_values_hbm, grad_keys_ref, grad_values_ref, out_sem
):
    chunks, lines = home_ref.shape[:2]
    capacity = lines // 2
    heads = grad_keys_ref.shape[2] // HD
    flat_ref = home_ref.reshape(chunks * lines, *home_ref.shape[2:])
    part = grad_keys_ref.shape[0] // PARTS
    stores = []
    for step in range(PARTS):

        def one_tile(offset, carry):
            tile = step * part + offset
            source = source_ref[tile]
            for head in range(heads):
                cols = slice(head * HD, (head + 1) * HD)
                grad_keys_ref[tile, :, cols] = flat_ref[source + lines * head]
                grad_values_ref[tile, :, cols] = flat_ref[source + lines * head + capacity]
            return carry

        lax.fori_loop(0, part, one_tile, 0, unroll=4)
        rows = pl.ds(step * part, part)
        for kind, (ref, hbm) in enumerate(
            ((grad_keys_ref, grad_keys_hbm), (grad_values_ref, grad_values_hbm))
        ):
            stores.append(
                pltpu.make_async_copy(ref.at[rows], hbm.at[rows], out_sem.at[kind, step])
            )
            stores[-1].start()
    for store in stores:
        store.wait()


def attend_backward(
    holder_ref,
    rank_ref,
    slot_ref,
    first_ref,
    steps_ref,
    bias_ref,
    recv_ref,
    queries_ref,
    dout_ref,
    back_hbm,
    grad_queries_ref,
    key_scr,
    value_scr,
    expo_scr,
    dprob_scr,
    top_scr,
    grad_key_scr,
    grad_value_scr,
    grad_query_scr,
    back_ref,
    out_sem,
):
    scale = 1.0 / math.sqrt(HD)
    rate = scale * math.log2(math.e)
    slots = bias_ref.shape[0]
    capacity = recv_ref.shape[1] // 2
    tile_len = TILE
    pieces = tile_len // recv_ref.shape[2]
    chunk, block = expo_scr.shape[1:]
    blocks = queries_ref.shape[0] // block
    group = grad_queries_ref.shape[1] // HD
    key_count = slots * tile_len
    tail = pl.ds(key_count, key_scr.shape[0] - key_count)
    contract_last = (((1,), (1,)), ((), ()))
    contract_inner = (((1,), (0,)), ((), ()))
    contract_first = (((0,), (0,)), ((), ()))

    def gather_slot(slot, carry):
        source = pl.ds(holder_ref[slot] * pieces, pieces)
        rank = rank_ref[slot]
        target = pl.ds(pl.multiple_of(slot * tile_len, tile_len), tile_len)
        key_scr[target, :HD] = recv_ref[source, rank].reshape(tile_len, HD)
        key_scr[target, HD:] = jnp.broadcast_to(bias_ref[pl.ds(slot, 1), :], (tile_len, HD)).astype(
            BF16
        )
        value_scr[target, :] = recv_ref[source, capacity + rank].reshape(tile_len, HD)
        return carry

    lax.fori_loop(0, slots, gather_slot, 0, unroll=8)
    key_scr[tail, :HD] = jnp.zeros((tail.size, HD), BF16)
    key_scr[tail, HD:] = jnp.full((tail.size, HD), HIDDEN, BF16)
    value_scr[tail, :] = jnp.zeros((tail.size, HD), BF16)
    grad_key_scr[...] = jnp.zeros_like(grad_key_scr)
    grad_value_scr[...] = jnp.zeros_like(grad_value_scr)

    def one_block(index, carry):
        rows = pl.ds(pl.multiple_of(index * block, block), block)
        first, steps = first_ref[index], steps_ref[index]

        def keys_of(step):
            return pl.ds(pl.multiple_of(first * tile_len + step * chunk, tile_len), chunk)

        def forward(step, carry):
            top, total, delta = carry
            where = keys_of(step)
            score = lax.dot_general(
                key_scr[where, :], queries_ref[rows, :], contract_last, preferred_element_type=F32
            )
            dprob = lax.dot_general(
                value_scr[where, :], dout_ref[rows, :], contract_last, preferred_element_type=F32
            )
            new_top = jnp.maximum(top, jnp.max(score, axis=0, keepdims=True))
            shrink = jnp.exp2((top - new_top) * rate)
            expo = jnp.exp2((score - new_top) * rate)
            expo_scr[step] = expo
            dprob_scr[step] = dprob
            top_scr[pl.ds(step, 1), :] = new_top
            return (
                new_top,
                total * shrink + jnp.sum(expo, axis=0, keepdims=True),
                delta * shrink + jnp.sum(expo * dprob, axis=0, keepdims=True),
            )

        zero = jnp.zeros((1, block), F32)
        top, total, delta = lax.fori_loop(
            0, steps, forward, (jnp.full((1, block), 2 * HIDDEN, F32), zero, zero)
        )
        inverse = 1.0 / total
        delta = delta * inverse

        def backward(step, grad_query):
            where = keys_of(step)
            factor = jnp.exp2((top_scr[pl.ds(step, 1), :] - top) * rate) * inverse
            prob = expo_scr[step] * factor
            dscore = (prob * (dprob_scr[step] - delta)).astype(BF16)
            grad_value_scr[where, :] += lax.dot_general(
                prob.astype(BF16), dout_ref[rows, :], contract_inner, preferred_element_type=F32
            )
            grad_key_scr[where, :] += lax.dot_general(
                dscore, queries_ref[rows, :HD], contract_inner, preferred_element_type=F32
            )
            return grad_query + lax.dot_general(
                dscore, key_scr[where, :HD], contract_first, preferred_element_type=F32
            )

        grad_query = lax.fori_loop(0, steps, backward, jnp.zeros((block, HD), F32))
        grad_query_scr[...] = grad_query * scale
        text_rows = pl.ds(pl.multiple_of(index * (block // group), block // group), block // group)
        for head in range(group):
            mine = grad_query_scr[pl.ds(head, block // group, stride=group), :]
            grad_queries_ref[text_rows, head * HD : (head + 1) * HD] = mine.astype(BF16)
        return carry

    lax.fori_loop(0, blocks, one_block, 0)

    part = slot_ref.shape[0] // PARTS
    stores = []
    for step in range(PARTS):

        def return_tiles(offset, carry):
            holder = step * part + offset

            def one_tile(rank):
                slot = jnp.maximum(slot_ref[holder, rank], 0)
                where = pl.ds(pl.multiple_of(slot * tile_len, tile_len), tile_len)
                chunks = pl.ds(holder * pieces, pieces)
                shape = (pieces, tile_len // pieces, HD)
                grad_key = (grad_key_scr[where, :] * scale).astype(BF16)
                back_ref[chunks, rank] = grad_key.reshape(shape)
                grad_value = grad_value_scr[where, :].astype(BF16)
                back_ref[chunks, capacity + rank] = grad_value.reshape(shape)

            for rank in range(capacity):
                one_tile(rank)
            return carry

        lax.fori_loop(0, part, return_tiles, 0, unroll=4)
        chunks = pl.ds(step * part * pieces, part * pieces)
        stores.append(
            pltpu.make_async_copy(back_ref.at[chunks], back_hbm.at[chunks], out_sem.at[step])
        )
        stores[-1].start()
    for store in stores:
        store.wait()


def prepare(queries, dout, tile_docs, tile_rows, doc_ends):
    rows = queries.shape[0]
    group = queries.shape[1] // HD
    docs = tile_docs[:, None] == jnp.arange(doc_ends.shape[0], dtype=jnp.int32)[None, :]
    slot_ends = jnp.sum(jnp.where(docs, doc_ends[None, :], 0), axis=1)
    slot_begins = jnp.sum(jnp.where(docs[:, 1:], doc_ends[None, :-1], 0), axis=1)
    text_row = jnp.arange(rows, dtype=jnp.int32)
    seen = (text_row[None, :] >= tile_rows[:, None]) & (text_row[None, :] < slot_ends[:, None])
    bias = jnp.where(seen, 0.0, HIDDEN).astype(F32)
    tile_len = TILE
    chunk_slots = CHUNK // tile_len
    block_begin = jnp.arange(rows * group // BLOCK, dtype=jnp.int32) * (BLOCK // group)
    first = jnp.sum((slot_ends[None, :] <= block_begin[:, None]).astype(jnp.int32), axis=1)
    until = jnp.sum(
        (slot_begins[None, :] < block_begin[:, None] + BLOCK // group).astype(jnp.int32), axis=1
    )
    steps = (until - first + chunk_slots - 1) // chunk_slots

    flat = rows * group
    query_rows = queries.reshape(flat, HD)
    dout_rows = dout.reshape(flat, HD)
    own_row = (jnp.arange(flat, dtype=jnp.int32) // group)[:, None] == text_row[None, :]
    query_rows = jnp.concatenate([query_rows, own_row.astype(BF16)], axis=1)

    return first, steps, bias, query_rows, dout_rows


def attention(recv, holder, rank, slot_of, first, steps, bias, query_rows, dout_rows):
    smem = pl.BlockSpec(memory_space=pltpu.SMEM)
    vmem = pl.BlockSpec(memory_space=pltpu.VMEM)
    slots, rows = bias.shape
    group = query_rows.shape[0] // rows
    key_count = slots * TILE
    return pl.pallas_call(
        attend_backward,
        out_shape=(
            jax.ShapeDtypeStruct(recv.shape, BF16),
            jax.ShapeDtypeStruct((rows, group * HD), BF16),
        ),
        in_specs=[smem] * 5 + [vmem] * 4,
        out_specs=(pl.BlockSpec(memory_space=pl.ANY), vmem),
        scratch_shapes=[
            pltpu.VMEM((key_count + CHUNK, 2 * HD), BF16),
            pltpu.VMEM((key_count + CHUNK, HD), BF16),
            pltpu.VMEM((key_count // CHUNK, CHUNK, BLOCK), F32),
            pltpu.VMEM((key_count // CHUNK, CHUNK, BLOCK), F32),
            pltpu.VMEM((key_count // CHUNK, BLOCK), F32),
            pltpu.VMEM((key_count + CHUNK, HD), F32),
            pltpu.VMEM((key_count + CHUNK, HD), F32),
            pltpu.VMEM((BLOCK, HD), F32),
            pltpu.VMEM(recv.shape, BF16),
            pltpu.SemaphoreType.DMA((PARTS,)),
        ],
        compiler_params=pltpu.CompilerParams(vmem_limit_bytes=VMEM_LIMIT),
        name="attend_backward",
    )(holder, rank, slot_of, first, steps, bias, recv, query_rows, dout_rows)


def per_device(queries, keys_in, values_in, dout, req_tiles, tile_docs, tile_rows, doc_ends):
    dp_count = lax.axis_size("dp")
    heads = lax.axis_size("tensor")
    slots = req_tiles.shape[0]
    capacity = slots // dp_count + 1
    row_part = keys_in.shape[1]
    rows = queries.shape[0]
    smem = pl.BlockSpec(memory_space=pltpu.SMEM)
    vmem = pl.BlockSpec(memory_space=pltpu.VMEM)
    hbm = pl.BlockSpec(memory_space=pl.ANY)
    params = pltpu.CompilerParams(vmem_limit_bytes=VMEM_LIMIT)

    holder = req_tiles // slots
    slot_index = jnp.arange(slots, dtype=jnp.int32)
    same_before = (holder[:, None] == holder[None, :]) & (slot_index[None, :] < slot_index[:, None])
    rank = jnp.sum(same_before.astype(jnp.int32), axis=1)
    places = jnp.arange(dp_count, dtype=jnp.int32)[:, None, None]
    ranks = jnp.arange(capacity, dtype=jnp.int32)[None, :, None]
    there = (holder[None, None, :] == places) & (rank[None, None, :] == ranks)
    asked = jnp.sum(jnp.where(there, (req_tiles % slots + 1)[None, None, :], 0), axis=-1) - 1
    slot_of = jnp.sum(jnp.where(there, (slot_index + 1)[None, None, :], 0), axis=-1) - 1
    asked = jnp.pad(asked, ((0, 0), (0, HD - capacity)))[:, None, :]
    wanted = lax.all_to_all(asked, "dp", split_axis=0, concat_axis=0, tiled=True)[:, :, :capacity]

    prepared = prepare(queries, dout, tile_docs, tile_rows, doc_ends)
    wanted, prepared = lax.optimization_barrier((wanted, prepared))

    send = pl.pallas_call(
        pick_tiles,
        out_shape=jax.ShapeDtypeStruct((dp_count * heads, 2 * capacity, row_part, HD), BF16),
        in_specs=[smem, hbm, hbm],
        out_specs=hbm,
        scratch_shapes=[
            pltpu.VMEM(keys_in.shape, BF16),
            pltpu.VMEM(values_in.shape, BF16),
            pltpu.VMEM((dp_count * heads, 2 * capacity, row_part, HD), BF16),
            pltpu.SemaphoreType.DMA((2,)),
            pltpu.SemaphoreType.DMA((PARTS,)),
        ],
        compiler_params=params,
        name="pick_tiles",
    )(wanted, keys_in, values_in)
    recv = lax.all_to_all(send, ("dp", "tensor"), split_axis=0, concat_axis=0, tiled=True)

    tile_index = jnp.arange(slots, dtype=jnp.int32)[:, None, None]
    lines = jnp.arange(dp_count, dtype=jnp.int32)[:, None] * (heads * 2 * capacity) + ranks[:, :, 0]
    source = jnp.sum(jnp.where(wanted[:, 0][None] == tile_index, lines[None], 0), axis=(1, 2))
    recv, source = lax.optimization_barrier((recv, source))
    back, grad_queries = attention(recv, holder, rank, slot_of, *prepared)

    home = lax.all_to_all(back, ("dp", "tensor"), split_axis=0, concat_axis=0, tiled=True)
    grad_keys, grad_values = pl.pallas_call(
        place_tiles,
        out_shape=(
            jax.ShapeDtypeStruct(keys_in.shape, BF16),
            jax.ShapeDtypeStruct(values_in.shape, BF16),
        ),
        in_specs=[smem, vmem],
        out_specs=(hbm, hbm),
        scratch_shapes=[
            pltpu.VMEM(keys_in.shape, BF16),
            pltpu.VMEM(values_in.shape, BF16),
            pltpu.SemaphoreType.DMA((2, PARTS)),
        ],
        compiler_params=params,
        name="place_tiles",
    )(source, home)
    return (grad_queries, grad_keys, grad_values)


def solution(mesh):
    return jax.shard_map(
        per_device,
        mesh=mesh,
        in_specs=(
            P("dp", "tensor"),
            P("dp", "tensor", None),
            P("dp", "tensor", None),
            P("dp", "tensor"),
            P("dp"),
            P("dp"),
            P("dp"),
            P("dp"),
        ),
        out_specs=(P("dp", "tensor"), P("dp", "tensor", None), P("dp", "tensor", None)),
        check_vma=False,
    )
```

```python
import math

import jax
import jax.numpy as jnp
from jax import lax
from jax.experimental import pallas as pl
from jax.experimental.pallas import tpu as pltpu
from jax.sharding import PartitionSpec as P

HD = 128
TILE = 16
BF16 = jnp.bfloat16
F32 = jnp.float32
HIDDEN = -1e30
CHUNK = 512
BLOCK = 256
PARTS = 4
VMEM_LIMIT = 48 * 1024 * 1024


def pick_tiles(
    wanted_ref, keys_hbm, values_hbm, send_hbm, keys_ref, values_ref, send_ref, in_sem, out_sem
):
    readers, _, capacity = wanted_ref.shape
    heads = keys_ref.shape[2] // HD
    loads = [
        pltpu.make_async_copy(keys_hbm, keys_ref, in_sem.at[0]),
        pltpu.make_async_copy(values_hbm, values_ref, in_sem.at[1]),
    ]
    for load in loads:
        load.start()
    for load in loads:
        load.wait()

    part = readers // PARTS
    stores = []
    for step in range(PARTS):

        def one_reader(offset, carry):
            reader = step * part + offset

            def one_tile(rank):
                tile = jnp.maximum(wanted_ref[reader, 0, rank], 0)
                for head in range(heads):
                    cols = slice(head * HD, (head + 1) * HD)
                    send_ref[reader * heads + head, rank] = keys_ref[tile, :, cols]
                    send_ref[reader * heads + head, capacity + rank] = values_ref[tile, :, cols]

            for rank in range(capacity):
                one_tile(rank)
            return carry

        lax.fori_loop(0, part, one_reader, 0, unroll=4)
        rows = pl.ds(step * part * heads, part * heads)
        stores.append(pltpu.make_async_copy(send_ref.at[rows], send_hbm.at[rows], out_sem.at[step]))
        stores[-1].start()
    for store in stores:
        store.wait()


def place_tiles(
    source_ref, home_ref, grad_keys_hbm, grad_values_hbm, grad_keys_ref, grad_values_ref, out_sem
):
    chunks, lines = home_ref.shape[:2]
    capacity = lines // 2
    heads = grad_keys_ref.shape[2] // HD
    flat_ref = home_ref.reshape(chunks * lines, *home_ref.shape[2:])
    part = grad_keys_ref.shape[0] // PARTS
    stores = []
    for step in range(PARTS):

        def one_tile(offset, carry):
            tile = step * part + offset
            source = source_ref[tile]
            for head in range(heads):
                cols = slice(head * HD, (head + 1) * HD)
                grad_keys_ref[tile, :, cols] = flat_ref[source + lines * head]
                grad_values_ref[tile, :, cols] = flat_ref[source + lines * head + capacity]
            return carry

        lax.fori_loop(0, part, one_tile, 0, unroll=4)
        rows = pl.ds(step * part, part)
        for kind, (ref, hbm) in enumerate(
            ((grad_keys_ref, grad_keys_hbm), (grad_values_ref, grad_values_hbm))
        ):
            stores.append(
                pltpu.make_async_copy(ref.at[rows], hbm.at[rows], out_sem.at[kind, step])
            )
            stores[-1].start()
    for store in stores:
        store.wait()


def attend_backward(
    holder_ref,
    rank_ref,
    slot_ref,
    first_ref,
    steps_ref,
    bias_ref,
    recv_ref,
    queries_ref,
    dout_ref,
    back_ref,
    grad_queries_ref,
    key_scr,
    value_scr,
    expo_scr,
    dprob_scr,
    top_scr,
    grad_key_scr,
    grad_value_scr,
):
    scale = 1.0 / math.sqrt(HD)
    rate = scale * math.log2(math.e)
    slots = bias_ref.shape[0]
    capacity = recv_ref.shape[1] // 2
    tile_len = TILE
    pieces = tile_len // recv_ref.shape[2]
    chunk, block = expo_scr.shape[1:]
    blocks = queries_ref.shape[0] // block
    group = grad_queries_ref.shape[1] // HD
    span = block // group
    key_count = slots * tile_len
    tail = pl.ds(key_count, key_scr.shape[0] - key_count)
    contract_last = (((1,), (1,)), ((), ()))
    contract_inner = (((1,), (0,)), ((), ()))
    contract_first = (((0,), (0,)), ((), ()))

    def gather_slot(slot, carry):
        source = pl.ds(holder_ref[slot] * pieces, pieces)
        rank = rank_ref[slot]
        target = pl.ds(pl.multiple_of(slot * tile_len, tile_len), tile_len)
        key_scr[target, :HD] = recv_ref[source, rank].reshape(tile_len, HD)
        key_scr[target, HD:] = jnp.broadcast_to(bias_ref[pl.ds(slot, 1), :], (tile_len, HD)).astype(
            BF16
        )
        value_scr[target, :] = recv_ref[source, capacity + rank].reshape(tile_len, HD)
        return carry

    lax.fori_loop(0, slots, gather_slot, 0, unroll=8)
    key_scr[tail, :HD] = jnp.zeros((tail.size, HD), BF16)
    key_scr[tail, HD:] = jnp.full((tail.size, HD), HIDDEN, BF16)
    value_scr[tail, :] = jnp.zeros((tail.size, HD), BF16)
    grad_key_scr[...] = jnp.zeros_like(grad_key_scr)
    grad_value_scr[...] = jnp.zeros_like(grad_value_scr)

    def one_block(index, carry):
        rows = pl.ds(pl.multiple_of(index * block, block), block)
        first, steps = first_ref[index], steps_ref[index]

        def keys_of(step):
            return pl.ds(pl.multiple_of(first * tile_len + step * chunk, tile_len), chunk)

        def forward(step, carry):
            top, total, delta = carry
            where = keys_of(step)
            score = lax.dot_general(
                key_scr[where, :], queries_ref[rows, :], contract_last, preferred_element_type=F32
            )
            dprob = lax.dot_general(
                value_scr[where, :], dout_ref[rows, :], contract_last, preferred_element_type=F32
            )
            new_top = jnp.maximum(top, jnp.max(score, axis=0, keepdims=True))
            shrink = jnp.exp2((top - new_top) * rate)
            expo = jnp.exp2((score - new_top) * rate)
            expo_scr[step] = expo
            dprob_scr[step] = dprob
            top_scr[pl.ds(step, 1), :] = new_top
            return (
                new_top,
                total * shrink + jnp.sum(expo, axis=0, keepdims=True),
                delta * shrink + jnp.sum(expo * dprob, axis=0, keepdims=True),
            )

        zero = jnp.zeros((1, block), F32)
        top, total, delta = lax.fori_loop(
            0, steps, forward, (jnp.full((1, block), 2 * HIDDEN, F32), zero, zero)
        )
        inverse = 1.0 / total
        delta = delta * inverse

        def backward(step, grad_query):
            where = keys_of(step)
            factor = jnp.exp2((top_scr[pl.ds(step, 1), :] - top) * rate) * inverse
            prob = expo_scr[step] * factor
            dscore = (prob * (dprob_scr[step] - delta)).astype(BF16)
            grad_value_scr[where, :] += lax.dot_general(
                prob.astype(BF16), dout_ref[rows, :], contract_inner, preferred_element_type=F32
            )
            grad_key_scr[where, :] += lax.dot_general(
                dscore, queries_ref[rows, :HD], contract_inner, preferred_element_type=F32
            )
            return grad_query + lax.dot_general(
                dscore, key_scr[where, :HD], contract_first, preferred_element_type=F32
            )

        grad_query = lax.fori_loop(0, steps, backward, jnp.zeros((block, HD), F32))
        grad_query = (grad_query * scale).astype(BF16)
        text_rows = pl.ds(pl.multiple_of(index * span, span), span)
        for head in range(group):
            mine = grad_query[head * span : (head + 1) * span]
            grad_queries_ref[text_rows, head * HD : (head + 1) * HD] = mine
        return carry

    lax.fori_loop(0, blocks, one_block, 0)

    def return_tiles(holder, carry):
        chunks = pl.ds(holder * pieces, pieces)
        shape = (pieces, tile_len // pieces, HD)
        for rank in range(capacity):
            slot = jnp.maximum(slot_ref[holder, rank], 0)
            where = pl.ds(pl.multiple_of(slot * tile_len, tile_len), tile_len)
            grad_key = (grad_key_scr[where, :] * scale).astype(BF16)
            back_ref[chunks, rank] = grad_key.reshape(shape)
            back_ref[chunks, capacity + rank] = grad_value_scr[where, :].astype(BF16).reshape(shape)
        return carry

    lax.fori_loop(0, slot_ref.shape[0], return_tiles, 0, unroll=4)


def by_block(rows, span):
    blocks = rows.reshape(rows.shape[0] // span, span, rows.shape[1] // HD, HD)
    return blocks.transpose(0, 2, 1, 3).reshape(-1, HD)


def prepare(queries, dout, tile_docs, tile_rows, doc_ends):
    rows = queries.shape[0]
    group = queries.shape[1] // HD
    docs = tile_docs[:, None] == jnp.arange(doc_ends.shape[0], dtype=jnp.int32)[None, :]
    slot_ends = jnp.sum(jnp.where(docs, doc_ends[None, :], 0), axis=1)
    slot_begins = jnp.sum(jnp.where(docs[:, 1:], doc_ends[None, :-1], 0), axis=1)
    text_row = jnp.arange(rows, dtype=jnp.int32)
    seen = (text_row[None, :] >= tile_rows[:, None]) & (text_row[None, :] < slot_ends[:, None])
    bias = jnp.where(seen, 0.0, HIDDEN).astype(F32)
    tile_len = TILE
    chunk_slots = CHUNK // tile_len
    block_begin = jnp.arange(rows * group // BLOCK, dtype=jnp.int32) * (BLOCK // group)
    first = jnp.sum((slot_ends[None, :] <= block_begin[:, None]).astype(jnp.int32), axis=1)
    until = jnp.sum(
        (slot_begins[None, :] < block_begin[:, None] + BLOCK // group).astype(jnp.int32), axis=1
    )
    steps = (until - first + chunk_slots - 1) // chunk_slots

    flat = rows * group
    span = BLOCK // group
    query_rows = by_block(queries, span)
    dout_rows = by_block(dout, span)
    position = jnp.arange(flat, dtype=jnp.int32)
    own = position // BLOCK * span + position % span
    own_row = own[:, None] == text_row[None, :]
    query_rows = jnp.concatenate([query_rows, own_row.astype(BF16)], axis=1)

    return first, steps, bias, query_rows, dout_rows


def attention(recv, holder, rank, slot_of, first, steps, bias, query_rows, dout_rows):
    smem = pl.BlockSpec(memory_space=pltpu.SMEM)
    vmem = pl.BlockSpec(memory_space=pltpu.VMEM)
    slots, rows = bias.shape
    group = query_rows.shape[0] // rows
    key_count = slots * TILE
    return pl.pallas_call(
        attend_backward,
        out_shape=(
            jax.ShapeDtypeStruct(recv.shape, BF16),
            jax.ShapeDtypeStruct((rows, group * HD), BF16),
        ),
        in_specs=[smem] * 5 + [vmem] * 4,
        out_specs=(vmem, vmem),
        scratch_shapes=[
            pltpu.VMEM((key_count + CHUNK, 2 * HD), BF16),
            pltpu.VMEM((key_count + CHUNK, HD), BF16),
            pltpu.VMEM((key_count // CHUNK, CHUNK, BLOCK), F32),
            pltpu.VMEM((key_count // CHUNK, CHUNK, BLOCK), F32),
            pltpu.VMEM((key_count // CHUNK, BLOCK), F32),
            pltpu.VMEM((key_count + CHUNK, HD), F32),
            pltpu.VMEM((key_count + CHUNK, HD), F32),
        ],
        compiler_params=pltpu.CompilerParams(vmem_limit_bytes=VMEM_LIMIT),
        name="attend_backward",
    )(holder, rank, slot_of, first, steps, bias, recv, query_rows, dout_rows)


def per_device(queries, keys_in, values_in, dout, req_tiles, tile_docs, tile_rows, doc_ends):
    dp_count = lax.axis_size("dp")
    heads = lax.axis_size("tensor")
    slots = req_tiles.shape[0]
    capacity = slots // dp_count + 1
    row_part = keys_in.shape[1]
    rows = queries.shape[0]
    smem = pl.BlockSpec(memory_space=pltpu.SMEM)
    vmem = pl.BlockSpec(memory_space=pltpu.VMEM)
    hbm = pl.BlockSpec(memory_space=pl.ANY)
    params = pltpu.CompilerParams(vmem_limit_bytes=VMEM_LIMIT)

    holder = req_tiles // slots
    slot_index = jnp.arange(slots, dtype=jnp.int32)
    same_before = (holder[:, None] == holder[None, :]) & (slot_index[None, :] < slot_index[:, None])
    rank = jnp.sum(same_before.astype(jnp.int32), axis=1)
    places = jnp.arange(dp_count, dtype=jnp.int32)[:, None, None]
    ranks = jnp.arange(capacity, dtype=jnp.int32)[None, :, None]
    there = (holder[None, None, :] == places) & (rank[None, None, :] == ranks)
    asked = jnp.sum(jnp.where(there, (req_tiles % slots + 1)[None, None, :], 0), axis=-1) - 1
    slot_of = jnp.sum(jnp.where(there, (slot_index + 1)[None, None, :], 0), axis=-1) - 1
    asked = jnp.pad(asked, ((0, 0), (0, HD - capacity)))[:, None, :]
    wanted = lax.all_to_all(asked, "dp", split_axis=0, concat_axis=0, tiled=True)[:, :, :capacity]

    prepared = prepare(queries, dout, tile_docs, tile_rows, doc_ends)
    wanted, prepared = lax.optimization_barrier((wanted, prepared))

    send = pl.pallas_call(
        pick_tiles,
        out_shape=jax.ShapeDtypeStruct((dp_count * heads, 2 * capacity, row_part, HD), BF16),
        in_specs=[smem, hbm, hbm],
        out_specs=hbm,
        scratch_shapes=[
            pltpu.VMEM(keys_in.shape, BF16),
            pltpu.VMEM(values_in.shape, BF16),
            pltpu.VMEM((dp_count * heads, 2 * capacity, row_part, HD), BF16),
            pltpu.SemaphoreType.DMA((2,)),
            pltpu.SemaphoreType.DMA((PARTS,)),
        ],
        compiler_params=params,
        name="pick_tiles",
    )(wanted, keys_in, values_in)
    recv = lax.all_to_all(send, ("dp", "tensor"), split_axis=0, concat_axis=0, tiled=True)

    tile_index = jnp.arange(slots, dtype=jnp.int32)[:, None, None]
    lines = jnp.arange(dp_count, dtype=jnp.int32)[:, None] * (heads * 2 * capacity) + ranks[:, :, 0]
    source = jnp.sum(jnp.where(wanted[:, 0][None] == tile_index, lines[None], 0), axis=(1, 2))
    recv, source = lax.optimization_barrier((recv, source))
    back, grad_queries = attention(recv, holder, rank, slot_of, *prepared)

    home = lax.all_to_all(back, ("dp", "tensor"), split_axis=0, concat_axis=0, tiled=True)
    grad_keys, grad_values = pl.pallas_call(
        place_tiles,
        out_shape=(
            jax.ShapeDtypeStruct(keys_in.shape, BF16),
            jax.ShapeDtypeStruct(values_in.shape, BF16),
        ),
        in_specs=[smem, vmem],
        out_specs=(hbm, hbm),
        scratch_shapes=[
            pltpu.VMEM(keys_in.shape, BF16),
            pltpu.VMEM(values_in.shape, BF16),
            pltpu.SemaphoreType.DMA((2, PARTS)),
        ],
        compiler_params=params,
        name="place_tiles",
    )(source, home)
    return (grad_queries, grad_keys, grad_values)


def solution(mesh):
    return jax.shard_map(
        per_device,
        mesh=mesh,
        in_specs=(
            P("dp", "tensor"),
            P("dp", "tensor", None),
            P("dp", "tensor", None),
            P("dp", "tensor"),
            P("dp"),
            P("dp"),
            P("dp"),
            P("dp"),
        ),
        out_specs=(P("dp", "tensor"), P("dp", "tensor", None), P("dp", "tensor", None)),
        check_vma=False,
    )
```

```python
import functools
import math

import jax
import jax.numpy as jnp
from jax import lax
from jax.experimental import pallas as pl
from jax.experimental.pallas import tpu as pltpu
from jax.sharding import PartitionSpec as P

HD = 128
TILE = 16
BF16 = jnp.bfloat16
F32 = jnp.float32
HIDDEN = -1e30
CHUNK = 512
BLOCK = 256
PARTS = 4
VMEM_LIMIT = 48 * 1024 * 1024


def ask(capacity, list_ref, asked_ref, rank_ref):
    holders, lanes = asked_ref.shape
    slots = list_ref.shape[1]
    tiles = list_ref[...]
    across = jnp.broadcast_to(tiles // slots, (slots, slots))
    slot_here = lax.broadcasted_iota(jnp.int32, (slots, slots), 1)
    slot_before = lax.broadcasted_iota(jnp.int32, (slots, slots), 0)
    before = (across.T == across) & (slot_before < slot_here)
    rank = jnp.sum(before.astype(jnp.int32), axis=0, keepdims=True)
    rank_ref[...] = rank
    holder = lax.broadcasted_iota(jnp.int32, (holders, slots), 0)
    lane = lax.broadcasted_iota(jnp.int32, (holders, lanes), 1)
    asked = jnp.full((holders, lanes), -1, jnp.int32)
    for step in range(capacity):
        mine = (across[:holders] == holder) & (rank == step)
        tile = jnp.sum(jnp.where(mine, tiles % slots + 1, 0), axis=1, keepdims=True) - 1
        asked = jnp.where(lane == step, tile, asked)
    asked_ref[...] = asked


def pick_tiles(
    wanted_ref, keys_hbm, values_hbm, send_hbm, keys_ref, values_ref, send_ref, in_sem, out_sem
):
    readers, _, capacity = wanted_ref.shape
    heads = keys_ref.shape[2] // HD
    loads = [
        pltpu.make_async_copy(keys_hbm, keys_ref, in_sem.at[0]),
        pltpu.make_async_copy(values_hbm, values_ref, in_sem.at[1]),
    ]
    for load in loads:
        load.start()
    for load in loads:
        load.wait()

    part = readers // PARTS
    stores = []
    for step in range(PARTS):

        def one_reader(offset, carry):
            reader = step * part + offset

            def one_tile(rank):
                tile = jnp.maximum(wanted_ref[reader, 0, rank], 0)
                for head in range(heads):
                    cols = slice(head * HD, (head + 1) * HD)
                    send_ref[reader * heads + head, rank] = keys_ref[tile, :, cols]
                    send_ref[reader * heads + head, capacity + rank] = values_ref[tile, :, cols]

            for rank in range(capacity):
                one_tile(rank)
            return carry

        lax.fori_loop(0, part, one_reader, 0, unroll=4)
        rows = pl.ds(step * part * heads, part * heads)
        stores.append(pltpu.make_async_copy(send_ref.at[rows], send_hbm.at[rows], out_sem.at[step]))
        stores[-1].start()
    for store in stores:
        store.wait()


def place_tiles(
    source_ref, home_ref, grad_keys_hbm, grad_values_hbm, grad_keys_ref, grad_values_ref, out_sem
):
    chunks, lines = home_ref.shape[:2]
    capacity = lines // 2
    heads = grad_keys_ref.shape[2] // HD
    flat_ref = home_ref.reshape(chunks * lines, *home_ref.shape[2:])
    part = grad_keys_ref.shape[0] // PARTS
    stores = []
    for step in range(PARTS):

        def one_tile(offset, carry):
            tile = step * part + offset
            source = source_ref[tile]
            for head in range(heads):
                cols = slice(head * HD, (head + 1) * HD)
                grad_keys_ref[tile, :, cols] = flat_ref[source + lines * head]
                grad_values_ref[tile, :, cols] = flat_ref[source + lines * head + capacity]
            return carry

        lax.fori_loop(0, part, one_tile, 0, unroll=4)
        rows = pl.ds(step * part, part)
        for kind, (ref, hbm) in enumerate(
            ((grad_keys_ref, grad_keys_hbm), (grad_values_ref, grad_values_hbm))
        ):
            stores.append(
                pltpu.make_async_copy(ref.at[rows], hbm.at[rows], out_sem.at[kind, step])
            )
            stores[-1].start()
    for store in stores:
        store.wait()


def attend_backward(
    holder_ref,
    rank_ref,
    first_ref,
    steps_ref,
    bias_ref,
    recv_ref,
    queries_ref,
    dout_ref,
    back_ref,
    grad_queries_hbm,
    key_scr,
    value_scr,
    expo_scr,
    dprob_scr,
    top_scr,
    grad_key_scr,
    grad_value_scr,
    grad_queries_ref,
    out_sem,
):
    scale = 1.0 / math.sqrt(HD)
    rate = scale * math.log2(math.e)
    slots = bias_ref.shape[0]
    capacity = recv_ref.shape[1] // 2
    tile_len = TILE
    pieces = tile_len // recv_ref.shape[2]
    chunk, block = expo_scr.shape[1:]
    blocks = queries_ref.shape[0] // block
    group = grad_queries_ref.shape[1] // HD
    span = block // group
    key_count = slots * tile_len
    tail = pl.ds(key_count, key_scr.shape[0] - key_count)
    contract_last = (((1,), (1,)), ((), ()))
    contract_inner = (((1,), (0,)), ((), ()))
    contract_first = (((0,), (0,)), ((), ()))

    def gather_slot(slot, carry):
        source = pl.ds(holder_ref[slot] * pieces, pieces)
        rank = rank_ref[slot]
        target = pl.ds(pl.multiple_of(slot * tile_len, tile_len), tile_len)
        key_scr[target, :HD] = recv_ref[source, rank].reshape(tile_len, HD)
        key_scr[target, HD:] = jnp.broadcast_to(bias_ref[pl.ds(slot, 1), :], (tile_len, HD)).astype(
            BF16
        )
        value_scr[target, :] = recv_ref[source, capacity + rank].reshape(tile_len, HD)
        return carry

    lax.fori_loop(0, slots, gather_slot, 0, unroll=8)
    key_scr[tail, :HD] = jnp.zeros((tail.size, HD), BF16)
    key_scr[tail, HD:] = jnp.full((tail.size, HD), HIDDEN, BF16)
    value_scr[tail, :] = jnp.zeros((tail.size, HD), BF16)
    grad_key_scr[...] = jnp.zeros_like(grad_key_scr)
    grad_value_scr[...] = jnp.zeros_like(grad_value_scr)

    def store_queries(index):
        text_rows = pl.ds(pl.multiple_of(index * span, span), span)
        return pltpu.make_async_copy(
            grad_queries_ref.at[text_rows], grad_queries_hbm.at[text_rows], out_sem.at[index]
        )

    def one_block(index, carry):
        rows = pl.ds(pl.multiple_of(index * block, block), block)
        first, steps = first_ref[index], steps_ref[index]

        def keys_of(step):
            return pl.ds(pl.multiple_of(first * tile_len + step * chunk, tile_len), chunk)

        def forward(step, carry):
            top, total, delta = carry
            where = keys_of(step)
            score = lax.dot_general(
                key_scr[where, :], queries_ref[rows, :], contract_last, preferred_element_type=F32
            )
            dprob = lax.dot_general(
                value_scr[where, :], dout_ref[rows, :], contract_last, preferred_element_type=F32
            )
            new_top = jnp.maximum(top, jnp.max(score, axis=0, keepdims=True))
            shrink = jnp.exp2((top - new_top) * rate)
            expo = jnp.exp2((score - new_top) * rate)
            expo_scr[step] = expo
            dprob_scr[step] = dprob
            top_scr[pl.ds(step, 1), :] = new_top
            return (
                new_top,
                total * shrink + jnp.sum(expo, axis=0, keepdims=True),
                delta * shrink + jnp.sum(expo * dprob, axis=0, keepdims=True),
            )

        zero = jnp.zeros((1, block), F32)
        top, total, delta = lax.fori_loop(
            0, steps, forward, (jnp.full((1, block), 2 * HIDDEN, F32), zero, zero)
        )
        inverse = 1.0 / total
        delta = delta * inverse

        def backward(step, grad_query):
            where = keys_of(step)
            factor = jnp.exp2((top_scr[pl.ds(step, 1), :] - top) * rate) * inverse
            prob = expo_scr[step] * factor
            dscore = (prob * (dprob_scr[step] - delta)).astype(BF16)
            grad_value_scr[where, :] += lax.dot_general(
                prob.astype(BF16), dout_ref[rows, :], contract_inner, preferred_element_type=F32
            )
            grad_key_scr[where, :] += lax.dot_general(
                dscore, queries_ref[rows, :HD], contract_inner, preferred_element_type=F32
            )
            return grad_query + lax.dot_general(
                dscore, key_scr[where, :HD], contract_first, preferred_element_type=F32
            )

        grad_query = lax.fori_loop(0, steps, backward, jnp.zeros((block, HD), F32))
        grad_query = (grad_query * scale).astype(BF16)
        text_rows = pl.ds(pl.multiple_of(index * span, span), span)
        for head in range(group):
            mine = grad_query[head * span : (head + 1) * span]
            grad_queries_ref[text_rows, head * HD : (head + 1) * HD] = mine
        store_queries(index).start()
        return carry

    lax.fori_loop(0, blocks, one_block, 0)

    def return_slot(slot, carry):
        source = pl.ds(holder_ref[slot] * pieces, pieces)
        rank = rank_ref[slot]
        where = pl.ds(pl.multiple_of(slot * tile_len, tile_len), tile_len)
        shape = (pieces, tile_len // pieces, HD)
        back_ref[source, rank] = (grad_key_scr[where, :] * scale).astype(BF16).reshape(shape)
        back_ref[source, capacity + rank] = grad_value_scr[where, :].astype(BF16).reshape(shape)
        return carry

    lax.fori_loop(0, slots, return_slot, 0, unroll=8)
    for index in range(blocks):
        store_queries(index).wait()


def by_block(rows, span):
    blocks = rows.reshape(rows.shape[0] // span, span, rows.shape[1] // HD, HD)
    return blocks.transpose(0, 2, 1, 3).reshape(-1, HD)


def prepare(queries, dout, tile_docs, tile_rows, doc_ends):
    rows = queries.shape[0]
    group = queries.shape[1] // HD
    docs = tile_docs[:, None] == jnp.arange(doc_ends.shape[0], dtype=jnp.int32)[None, :]
    slot_ends = jnp.sum(jnp.where(docs, doc_ends[None, :], 0), axis=1)
    slot_begins = jnp.sum(jnp.where(docs[:, 1:], doc_ends[None, :-1], 0), axis=1)
    text_row = jnp.arange(rows, dtype=jnp.int32)
    seen = (text_row[None, :] >= tile_rows[:, None]) & (text_row[None, :] < slot_ends[:, None])
    bias = jnp.where(seen, 0.0, HIDDEN).astype(F32)
    tile_len = TILE
    chunk_slots = CHUNK // tile_len
    block_begin = jnp.arange(rows * group // BLOCK, dtype=jnp.int32) * (BLOCK // group)
    first = jnp.sum((slot_ends[None, :] <= block_begin[:, None]).astype(jnp.int32), axis=1)
    until = jnp.sum(
        (slot_begins[None, :] < block_begin[:, None] + BLOCK // group).astype(jnp.int32), axis=1
    )
    steps = (until - first + chunk_slots - 1) // chunk_slots

    flat = rows * group
    span = BLOCK // group
    query_rows = by_block(queries, span)
    dout_rows = by_block(dout, span)
    position = jnp.arange(flat, dtype=jnp.int32)
    own = position // BLOCK * span + position % span
    own_row = own[:, None] == text_row[None, :]
    query_rows = jnp.concatenate([query_rows, own_row.astype(BF16)], axis=1)

    return first, steps, bias, query_rows, dout_rows


def attention(recv, holder, rank, first, steps, bias, query_rows, dout_rows):
    smem = pl.BlockSpec(memory_space=pltpu.SMEM)
    vmem = pl.BlockSpec(memory_space=pltpu.VMEM)
    slots, rows = bias.shape
    group = query_rows.shape[0] // rows
    key_count = slots * TILE
    return pl.pallas_call(
        attend_backward,
        out_shape=(
            jax.ShapeDtypeStruct(recv.shape, BF16),
            jax.ShapeDtypeStruct((rows, group * HD), BF16),
        ),
        in_specs=[smem] * 4 + [vmem] * 4,
        out_specs=(vmem, pl.BlockSpec(memory_space=pl.ANY)),
        scratch_shapes=[
            pltpu.VMEM((key_count + CHUNK, 2 * HD), BF16),
            pltpu.VMEM((key_count + CHUNK, HD), BF16),
            pltpu.VMEM((-(-key_count // CHUNK), CHUNK, BLOCK), F32),
            pltpu.VMEM((-(-key_count // CHUNK), CHUNK, BLOCK), F32),
            pltpu.VMEM((-(-key_count // CHUNK), BLOCK), F32),
            pltpu.VMEM((key_count + CHUNK, HD), F32),
            pltpu.VMEM((key_count + CHUNK, HD), F32),
            pltpu.VMEM((rows, group * HD), BF16),
            pltpu.SemaphoreType.DMA((rows * group // BLOCK,)),
        ],
        compiler_params=pltpu.CompilerParams(vmem_limit_bytes=VMEM_LIMIT),
        name="attend_backward",
    )(holder, rank, first, steps, bias, recv, query_rows, dout_rows)


def per_device(queries, keys_in, values_in, dout, req_tiles, tile_docs, tile_rows, doc_ends):
    dp_count = lax.axis_size("dp")
    heads = lax.axis_size("tensor")
    slots = req_tiles.shape[0]
    capacity = slots // dp_count + 1
    row_part = keys_in.shape[1]
    rows = queries.shape[0]
    smem = pl.BlockSpec(memory_space=pltpu.SMEM)
    vmem = pl.BlockSpec(memory_space=pltpu.VMEM)
    hbm = pl.BlockSpec(memory_space=pl.ANY)
    params = pltpu.CompilerParams(vmem_limit_bytes=VMEM_LIMIT)

    asked, rank = pl.pallas_call(
        functools.partial(ask, capacity),
        out_shape=(
            jax.ShapeDtypeStruct((dp_count, HD), jnp.int32),
            jax.ShapeDtypeStruct((1, slots), jnp.int32),
        ),
        in_specs=[vmem],
        out_specs=(vmem, vmem),
        name="ask",
    )(req_tiles.reshape(1, slots))
    holder, rank = req_tiles // slots, rank.reshape(slots)
    asked = asked[:, None, :]
    ranks = jnp.arange(capacity, dtype=jnp.int32)[None, :, None]
    wanted = lax.all_to_all(asked, "dp", split_axis=0, concat_axis=0, tiled=True)[:, :, :capacity]

    prepared = prepare(queries, dout, tile_docs, tile_rows, doc_ends)
    wanted, prepared = lax.optimization_barrier((wanted, prepared))

    send = pl.pallas_call(
        pick_tiles,
        out_shape=jax.ShapeDtypeStruct((dp_count * heads, 2 * capacity, row_part, HD), BF16),
        in_specs=[smem, hbm, hbm],
        out_specs=hbm,
        scratch_shapes=[
            pltpu.VMEM(keys_in.shape, BF16),
            pltpu.VMEM(values_in.shape, BF16),
            pltpu.VMEM((dp_count * heads, 2 * capacity, row_part, HD), BF16),
            pltpu.SemaphoreType.DMA((2,)),
            pltpu.SemaphoreType.DMA((PARTS,)),
        ],
        compiler_params=params,
        name="pick_tiles",
    )(wanted, keys_in, values_in)
    recv = lax.all_to_all(send, ("dp", "tensor"), split_axis=0, concat_axis=0, tiled=True)

    tile_index = jnp.arange(slots, dtype=jnp.int32)[:, None, None]
    lines = jnp.arange(dp_count, dtype=jnp.int32)[:, None] * (heads * 2 * capacity) + ranks[:, :, 0]
    source = jnp.sum(jnp.where(wanted[:, 0][None] == tile_index, lines[None], 0), axis=(1, 2))
    recv, source = lax.optimization_barrier((recv, source))
    back, grad_queries = attention(recv, holder, rank, *prepared)

    home = lax.all_to_all(back, ("dp", "tensor"), split_axis=0, concat_axis=0, tiled=True)
    grad_keys, grad_values = pl.pallas_call(
        place_tiles,
        out_shape=(
            jax.ShapeDtypeStruct(keys_in.shape, BF16),
            jax.ShapeDtypeStruct(values_in.shape, BF16),
        ),
        in_specs=[smem, vmem],
        out_specs=(hbm, hbm),
        scratch_shapes=[
            pltpu.VMEM(keys_in.shape, BF16),
            pltpu.VMEM(values_in.shape, BF16),
            pltpu.SemaphoreType.DMA((2, PARTS)),
        ],
        compiler_params=params,
        name="place_tiles",
    )(source, home)
    return (grad_queries, grad_keys, grad_values)


def solution(mesh):
    return jax.shard_map(
        per_device,
        mesh=mesh,
        in_specs=(
            P("dp", "tensor"),
            P("dp", "tensor", None),
            P("dp", "tensor", None),
            P("dp", "tensor"),
            P("dp"),
            P("dp"),
            P("dp"),
            P("dp"),
        ),
        out_specs=(P("dp", "tensor"), P("dp", "tensor", None), P("dp", "tensor", None)),
        check_vma=False,
    )
```

```python
import functools
import math

import jax
import jax.numpy as jnp
from jax import lax
from jax.experimental import pallas as pl
from jax.experimental.pallas import tpu as pltpu
from jax.sharding import PartitionSpec as P

HD = 128
TILE = 16
BF16 = jnp.bfloat16
F32 = jnp.float32
HIDDEN = -1e30
CHUNK = 768
BLOCK = 256
PARTS = 8
VMEM_LIMIT = 48 * 1024 * 1024


def ask(capacity, list_ref, asked_ref, rank_ref):
    holders, lanes = asked_ref.shape
    slots = list_ref.shape[1]
    tiles = list_ref[...]
    across = jnp.broadcast_to(tiles // slots, (slots, slots))
    slot_here = lax.broadcasted_iota(jnp.int32, (slots, slots), 1)
    slot_before = lax.broadcasted_iota(jnp.int32, (slots, slots), 0)
    before = (across.T == across) & (slot_before < slot_here)
    rank = jnp.sum(before.astype(jnp.int32), axis=0, keepdims=True)
    rank_ref[...] = rank
    holder = lax.broadcasted_iota(jnp.int32, (holders, slots), 0)
    lane = lax.broadcasted_iota(jnp.int32, (holders, lanes), 1)
    asked = jnp.full((holders, lanes), -1, jnp.int32)
    for step in range(capacity):
        mine = (across[:holders] == holder) & (rank == step)
        tile = jnp.sum(jnp.where(mine, tiles % slots + 1, 0), axis=1, keepdims=True) - 1
        asked = jnp.where(lane == step, tile, asked)
    asked_ref[...] = asked


def pick_tiles(
    wanted_ref, keys_ref, values_ref, send_hbm, send_ref, out_sem
):
    readers, _, capacity = wanted_ref.shape
    heads = keys_ref.shape[2] // HD
    part = readers // PARTS
    stores = []
    for step in range(PARTS):

        def one_reader(offset, carry):
            reader = step * part + offset

            def one_tile(rank):
                tile = jnp.maximum(wanted_ref[reader, 0, rank], 0)
                for head in range(heads):
                    cols = slice(head * HD, (head + 1) * HD)
                    send_ref[reader * heads + head, rank] = keys_ref[tile, :, cols]
                    send_ref[reader * heads + head, capacity + rank] = values_ref[tile, :, cols]

            for rank in range(capacity):
                one_tile(rank)
            return carry

        lax.fori_loop(0, part, one_reader, 0, unroll=4)
        rows = pl.ds(step * part * heads, part * heads)
        stores.append(pltpu.make_async_copy(send_ref.at[rows], send_hbm.at[rows], out_sem.at[step]))
        stores[-1].start()
    for store in stores:
        store.wait()


def place_tiles(
    source_ref, home_ref, grad_keys_hbm, grad_values_hbm, grad_keys_ref, grad_values_ref, out_sem
):
    chunks, lines = home_ref.shape[:2]
    capacity = lines // 2
    heads = grad_keys_ref.shape[2] // HD
    flat_ref = home_ref.reshape(chunks * lines, *home_ref.shape[2:])
    part = grad_keys_ref.shape[0] // PARTS
    stores = []
    for step in range(PARTS):

        def one_tile(offset, carry):
            tile = step * part + offset
            source = source_ref[tile]
            for head in range(heads):
                cols = slice(head * HD, (head + 1) * HD)
                grad_keys_ref[tile, :, cols] = flat_ref[source + lines * head]
                grad_values_ref[tile, :, cols] = flat_ref[source + lines * head + capacity]
            return carry

        lax.fori_loop(0, part, one_tile, 0, unroll=4)
        rows = pl.ds(step * part, part)
        for kind, (ref, hbm) in enumerate(
            ((grad_keys_ref, grad_keys_hbm), (grad_values_ref, grad_values_hbm))
        ):
            stores.append(
                pltpu.make_async_copy(ref.at[rows], hbm.at[rows], out_sem.at[kind, step])
            )
            stores[-1].start()
    for store in stores:
        store.wait()


def attend_backward(
    holder_ref,
    rank_ref,
    first_ref,
    steps_ref,
    bias_ref,
    recv_ref,
    queries_ref,
    dout_ref,
    back_ref,
    grad_queries_hbm,
    key_scr,
    value_scr,
    expo_scr,
    dprob_scr,
    top_scr,
    grad_key_scr,
    grad_value_scr,
    grad_queries_ref,
    out_sem,
):
    scale = 1.0 / math.sqrt(HD)
    rate = scale * math.log2(math.e)
    slots = bias_ref.shape[0]
    capacity = recv_ref.shape[1] // 2
    tile_len = TILE
    pieces = tile_len // recv_ref.shape[2]
    chunk, block = expo_scr.shape[1:]
    blocks = queries_ref.shape[0] // block
    group = grad_queries_ref.shape[1] // HD
    span = block // group
    key_count = slots * tile_len
    tail = pl.ds(key_count, key_scr.shape[0] - key_count)
    contract_last = (((1,), (1,)), ((), ()))
    contract_inner = (((1,), (0,)), ((), ()))
    contract_first = (((0,), (0,)), ((), ()))

    def gather_slot(slot, carry):
        source = pl.ds(holder_ref[slot] * pieces, pieces)
        rank = rank_ref[slot]
        target = pl.ds(pl.multiple_of(slot * tile_len, tile_len), tile_len)
        key_scr[target, :HD] = recv_ref[source, rank].reshape(tile_len, HD)
        key_scr[target, HD:] = jnp.broadcast_to(bias_ref[pl.ds(slot, 1), :], (tile_len, HD)).astype(
            BF16
        )
        value_scr[target, :] = recv_ref[source, capacity + rank].reshape(tile_len, HD)
        grad_key_scr[target, :] = jnp.zeros((tile_len, HD), F32)
        grad_value_scr[target, :] = jnp.zeros((tile_len, HD), F32)
        return carry

    lax.fori_loop(0, slots, gather_slot, 0, unroll=8)
    key_scr[tail, :HD] = jnp.zeros((tail.size, HD), BF16)
    key_scr[tail, HD:] = jnp.full((tail.size, HD), HIDDEN, BF16)
    value_scr[tail, :] = jnp.zeros((tail.size, HD), BF16)
    grad_key_scr[tail, :] = jnp.zeros((tail.size, HD), F32)
    grad_value_scr[tail, :] = jnp.zeros((tail.size, HD), F32)

    def store_queries(index):
        text_rows = pl.ds(pl.multiple_of(index * span, span), span)
        return pltpu.make_async_copy(
            grad_queries_ref.at[text_rows], grad_queries_hbm.at[text_rows], out_sem.at[index]
        )

    def one_block(index, carry):
        rows = pl.ds(pl.multiple_of(index * block, block), block)
        first, steps = first_ref[index], steps_ref[index]

        def keys_of(step):
            return pl.ds(pl.multiple_of(first * tile_len + step * chunk, tile_len), chunk)

        def forward(step, carry):
            top, total, delta = carry
            where = keys_of(step)
            score = lax.dot_general(
                key_scr[where, :], queries_ref[rows, :], contract_last, preferred_element_type=F32
            )
            dprob = lax.dot_general(
                value_scr[where, :], dout_ref[rows, :], contract_last, preferred_element_type=F32
            )
            new_top = jnp.maximum(top, jnp.max(score, axis=0, keepdims=True))
            shrink = jnp.exp2((top - new_top) * rate)
            expo = jnp.exp2((score - new_top) * rate)
            expo_scr[step] = expo
            dprob_scr[step] = dprob
            top_scr[pl.ds(step, 1), :] = new_top
            return (
                new_top,
                total * shrink + jnp.sum(expo, axis=0, keepdims=True),
                delta * shrink + jnp.sum(expo * dprob, axis=0, keepdims=True),
            )

        zero = jnp.zeros((1, block), F32)
        top, total, delta = lax.fori_loop(
            0, steps, forward, (jnp.full((1, block), 2 * HIDDEN, F32), zero, zero)
        )
        inverse = 1.0 / total
        delta = delta * inverse

        def backward(step, grad_query):
            where = keys_of(step)
            factor = jnp.exp2((top_scr[pl.ds(step, 1), :] - top) * rate) * inverse
            prob = expo_scr[step] * factor
            dscore = (prob * (dprob_scr[step] - delta)).astype(BF16)
            grad_value_scr[where, :] += lax.dot_general(
                prob.astype(BF16), dout_ref[rows, :], contract_inner, preferred_element_type=F32
            )
            grad_key_scr[where, :] += lax.dot_general(
                dscore, queries_ref[rows, :HD], contract_inner, preferred_element_type=F32
            )
            return grad_query + lax.dot_general(
                dscore, key_scr[where, :HD], contract_first, preferred_element_type=F32
            )

        grad_query = lax.fori_loop(0, steps, backward, jnp.zeros((block, HD), F32))
        grad_query = (grad_query * scale).astype(BF16)
        text_rows = pl.ds(pl.multiple_of(index * span, span), span)
        for head in range(group):
            mine = grad_query[head * span : (head + 1) * span]
            grad_queries_ref[text_rows, head * HD : (head + 1) * HD] = mine
        store_queries(index).start()
        return carry

    lax.fori_loop(0, blocks, one_block, 0)

    def return_slot(slot, carry):
        source = pl.ds(holder_ref[slot] * pieces, pieces)
        rank = rank_ref[slot]
        where = pl.ds(pl.multiple_of(slot * tile_len, tile_len), tile_len)
        shape = (pieces, tile_len // pieces, HD)
        back_ref[source, rank] = (grad_key_scr[where, :] * scale).astype(BF16).reshape(shape)
        back_ref[source, capacity + rank] = grad_value_scr[where, :].astype(BF16).reshape(shape)
        return carry

    lax.fori_loop(0, slots, return_slot, 0, unroll=8)
    for index in range(blocks):
        store_queries(index).wait()


def by_block(rows, span):
    blocks = rows.reshape(rows.shape[0] // span, span, rows.shape[1] // HD, HD)
    return blocks.transpose(0, 2, 1, 3).reshape(-1, HD)


def prepare(queries, dout, tile_docs, tile_rows, doc_ends):
    rows = queries.shape[0]
    group = queries.shape[1] // HD
    docs = tile_docs[:, None] == jnp.arange(doc_ends.shape[0], dtype=jnp.int32)[None, :]
    slot_ends = jnp.sum(jnp.where(docs, doc_ends[None, :], 0), axis=1)
    slot_begins = jnp.sum(jnp.where(docs[:, 1:], doc_ends[None, :-1], 0), axis=1)
    text_row = jnp.arange(rows, dtype=jnp.int32)
    seen = (text_row[None, :] >= tile_rows[:, None]) & (text_row[None, :] < slot_ends[:, None])
    bias = jnp.where(seen, 0.0, HIDDEN).astype(F32)
    tile_len = TILE
    chunk_slots = CHUNK // tile_len
    block_begin = jnp.arange(rows * group // BLOCK, dtype=jnp.int32) * (BLOCK // group)
    first = jnp.sum((slot_ends[None, :] <= block_begin[:, None]).astype(jnp.int32), axis=1)
    until = jnp.sum(
        (slot_begins[None, :] < block_begin[:, None] + BLOCK // group).astype(jnp.int32), axis=1
    )
    steps = (until - first + chunk_slots - 1) // chunk_slots

    flat = rows * group
    span = BLOCK // group
    query_rows = by_block(queries, span)
    dout_rows = by_block(dout, span)
    position = jnp.arange(flat, dtype=jnp.int32)
    own = position // BLOCK * span + position % span
    own_row = own[:, None] == text_row[None, :]
    query_rows = jnp.concatenate([query_rows, own_row.astype(BF16)], axis=1)

    return first, steps, bias, query_rows, dout_rows


def attention(recv, holder, rank, first, steps, bias, query_rows, dout_rows):
    smem = pl.BlockSpec(memory_space=pltpu.SMEM)
    vmem = pl.BlockSpec(memory_space=pltpu.VMEM)
    slots, rows = bias.shape
    group = query_rows.shape[0] // rows
    key_count = slots * TILE
    return pl.pallas_call(
        attend_backward,
        out_shape=(
            jax.ShapeDtypeStruct(recv.shape, BF16),
            jax.ShapeDtypeStruct((rows, group * HD), BF16),
        ),
        in_specs=[smem] * 4 + [vmem] * 4,
        out_specs=(vmem, pl.BlockSpec(memory_space=pl.ANY)),
        scratch_shapes=[
            pltpu.VMEM((key_count + CHUNK, 2 * HD), BF16),
            pltpu.VMEM((key_count + CHUNK, HD), BF16),
            pltpu.VMEM((-(-key_count // CHUNK), CHUNK, BLOCK), F32),
            pltpu.VMEM((-(-key_count // CHUNK), CHUNK, BLOCK), F32),
            pltpu.VMEM((-(-key_count // CHUNK), BLOCK), F32),
            pltpu.VMEM((key_count + CHUNK, HD), F32),
            pltpu.VMEM((key_count + CHUNK, HD), F32),
            pltpu.VMEM((rows, group * HD), BF16),
            pltpu.SemaphoreType.DMA((rows * group // BLOCK,)),
        ],
        compiler_params=pltpu.CompilerParams(vmem_limit_bytes=VMEM_LIMIT),
        name="attend_backward",
    )(holder, rank, first, steps, bias, recv, query_rows, dout_rows)


def per_device(queries, keys_in, values_in, dout, req_tiles, tile_docs, tile_rows, doc_ends):
    dp_count = lax.axis_size("dp")
    heads = lax.axis_size("tensor")
    slots = req_tiles.shape[0]
    capacity = slots // dp_count + 1
    row_part = keys_in.shape[1]
    rows = queries.shape[0]
    smem = pl.BlockSpec(memory_space=pltpu.SMEM)
    vmem = pl.BlockSpec(memory_space=pltpu.VMEM)
    hbm = pl.BlockSpec(memory_space=pl.ANY)
    params = pltpu.CompilerParams(vmem_limit_bytes=VMEM_LIMIT)

    asked, rank = pl.pallas_call(
        functools.partial(ask, capacity),
        out_shape=(
            jax.ShapeDtypeStruct((dp_count, HD), jnp.int32),
            jax.ShapeDtypeStruct((1, slots), jnp.int32),
        ),
        in_specs=[vmem],
        out_specs=(vmem, vmem),
        name="ask",
    )(req_tiles.reshape(1, slots))
    holder, rank = req_tiles // slots, rank.reshape(slots)
    asked = asked[:, None, :]
    ranks = jnp.arange(capacity, dtype=jnp.int32)[None, :, None]
    wanted = lax.all_to_all(asked, "dp", split_axis=0, concat_axis=0, tiled=True)[:, :, :capacity]

    prepared = prepare(queries, dout, tile_docs, tile_rows, doc_ends)
    wanted, prepared = lax.optimization_barrier((wanted, prepared))

    send = pl.pallas_call(
        pick_tiles,
        out_shape=jax.ShapeDtypeStruct((dp_count * heads, 2 * capacity, row_part, HD), BF16),
        in_specs=[smem, vmem, vmem],
        out_specs=hbm,
        scratch_shapes=[
            pltpu.VMEM((dp_count * heads, 2 * capacity, row_part, HD), BF16),
            pltpu.SemaphoreType.DMA((PARTS,)),
        ],
        compiler_params=params,
        name="pick_tiles",
    )(wanted, keys_in, values_in)
    recv = lax.all_to_all(send, ("dp", "tensor"), split_axis=0, concat_axis=0, tiled=True)

    tile_index = jnp.arange(slots, dtype=jnp.int32)[:, None, None]
    lines = jnp.arange(dp_count, dtype=jnp.int32)[:, None] * (heads * 2 * capacity) + ranks[:, :, 0]
    source = jnp.sum(jnp.where(wanted[:, 0][None] == tile_index, lines[None], 0), axis=(1, 2))
    recv, source = lax.optimization_barrier((recv, source))
    back, grad_queries = attention(recv, holder, rank, *prepared)

    home = lax.all_to_all(back, ("dp", "tensor"), split_axis=0, concat_axis=0, tiled=True)
    grad_keys, grad_values = pl.pallas_call(
        place_tiles,
        out_shape=(
            jax.ShapeDtypeStruct(keys_in.shape, BF16),
            jax.ShapeDtypeStruct(values_in.shape, BF16),
        ),
        in_specs=[smem, vmem],
        out_specs=(hbm, hbm),
        scratch_shapes=[
            pltpu.VMEM(keys_in.shape, BF16),
            pltpu.VMEM(values_in.shape, BF16),
            pltpu.SemaphoreType.DMA((2, PARTS)),
        ],
        compiler_params=params,
        name="place_tiles",
    )(source, home)
    return (grad_queries, grad_keys, grad_values)


def solution(mesh):
    return jax.shard_map(
        per_device,
        mesh=mesh,
        in_specs=(
            P("dp", "tensor"),
            P("dp", "tensor", None),
            P("dp", "tensor", None),
            P("dp", "tensor"),
            P("dp"),
            P("dp"),
            P("dp"),
            P("dp"),
        ),
        out_specs=(P("dp", "tensor"), P("dp", "tensor", None), P("dp", "tensor", None)),
        check_vma=False,
    )
```

```python
import functools
import math

import jax
import jax.numpy as jnp
from jax import lax
from jax.experimental import pallas as pl
from jax.experimental.pallas import tpu as pltpu
from jax.sharding import PartitionSpec as P

HD = 128
TILE = 16
BF16 = jnp.bfloat16
F32 = jnp.float32
HIDDEN = -1e30
CHUNK = 768
BLOCK = 256
PARTS = 8
VMEM_LIMIT = 48 * 1024 * 1024


def ask(capacity, list_ref, asked_ref, rank_ref, holder_ref):
    holders, lanes = asked_ref.shape
    slots = list_ref.shape[1]
    tiles = list_ref[...]
    across = jnp.broadcast_to(tiles // slots, (slots, slots))
    slot_here = lax.broadcasted_iota(jnp.int32, (slots, slots), 1)
    slot_before = lax.broadcasted_iota(jnp.int32, (slots, slots), 0)
    before = (across.T == across) & (slot_before < slot_here)
    rank = jnp.sum(before.astype(jnp.int32), axis=0, keepdims=True)
    rank_ref[...] = rank
    holder_ref[...] = tiles // slots
    holder = lax.broadcasted_iota(jnp.int32, (holders, slots), 0)
    lane = lax.broadcasted_iota(jnp.int32, (holders, lanes), 1)
    asked = jnp.full((holders, lanes), -1, jnp.int32)
    for step in range(capacity):
        mine = (across[:holders] == holder) & (rank == step)
        tile = jnp.sum(jnp.where(mine, tiles % slots + 1, 0), axis=1, keepdims=True) - 1
        asked = jnp.where(lane == step, tile, asked)
    asked_ref[...] = asked


def pick_tiles(wanted_ref, keys_ref, values_ref, send_ref):
    readers, _, capacity = wanted_ref.shape
    heads = keys_ref.shape[2] // HD
    def one_reader(reader, carry):
        for rank in range(capacity):
            tile = jnp.maximum(wanted_ref[reader, 0, rank], 0)
            for head in range(heads):
                cols = slice(head * HD, (head + 1) * HD)
                send_ref[reader * heads + head, rank] = keys_ref[tile, :, cols]
                send_ref[reader * heads + head, capacity + rank] = values_ref[tile, :, cols]
        return carry

    lax.fori_loop(0, readers, one_reader, 0, unroll=4)


def place_tiles(
    source_ref, home_ref, grad_keys_hbm, grad_values_hbm, grad_keys_ref, grad_values_ref, out_sem
):
    chunks, lines = home_ref.shape[:2]
    capacity = lines // 2
    heads = grad_keys_ref.shape[2] // HD
    flat_ref = home_ref.reshape(chunks * lines, *home_ref.shape[2:])
    part = grad_keys_ref.shape[0] // PARTS
    stores = []
    for step in range(PARTS):

        def one_tile(offset, carry):
            tile = step * part + offset
            source = source_ref[tile]
            for head in range(heads):
                cols = slice(head * HD, (head + 1) * HD)
                grad_keys_ref[tile, :, cols] = flat_ref[source + lines * head]
                grad_values_ref[tile, :, cols] = flat_ref[source + lines * head + capacity]
            return carry

        lax.fori_loop(0, part, one_tile, 0, unroll=4)
        rows = pl.ds(step * part, part)
        for kind, (ref, hbm) in enumerate(
            ((grad_keys_ref, grad_keys_hbm), (grad_values_ref, grad_values_hbm))
        ):
            stores.append(
                pltpu.make_async_copy(ref.at[rows], hbm.at[rows], out_sem.at[kind, step])
            )
            stores[-1].start()
    for store in stores:
        store.wait()


def attend_backward(
    holder_ref,
    rank_ref,
    first_ref,
    steps_ref,
    bias_ref,
    recv_ref,
    queries_ref,
    dout_ref,
    back_ref,
    grad_queries_hbm,
    key_scr,
    value_scr,
    expo_scr,
    dprob_scr,
    top_scr,
    grad_key_scr,
    grad_value_scr,
    grad_queries_ref,
    out_sem,
):
    scale = 1.0 / math.sqrt(HD)
    rate = scale * math.log2(math.e)
    slots = bias_ref.shape[0]
    capacity = recv_ref.shape[1] // 2
    tile_len = TILE
    pieces = tile_len // recv_ref.shape[2]
    chunk, block = expo_scr.shape[1:]
    blocks = queries_ref.shape[0] // block
    group = grad_queries_ref.shape[1] // HD
    span = block // group
    key_count = slots * tile_len
    tail = pl.ds(key_count, key_scr.shape[0] - key_count)
    contract_last = (((1,), (1,)), ((), ()))
    contract_inner = (((1,), (0,)), ((), ()))
    contract_first = (((0,), (0,)), ((), ()))

    def gather_slot(slot, carry):
        source = pl.ds(holder_ref[slot] * pieces, pieces)
        rank = rank_ref[slot]
        target = pl.ds(pl.multiple_of(slot * tile_len, tile_len), tile_len)
        key_scr[target, :HD] = recv_ref[source, rank].reshape(tile_len, HD)
        key_scr[target, HD:] = jnp.broadcast_to(bias_ref[pl.ds(slot, 1), :], (tile_len, HD)).astype(
            BF16
        )
        value_scr[target, :] = recv_ref[source, capacity + rank].reshape(tile_len, HD)
        grad_key_scr[target, :] = jnp.zeros((tile_len, HD), F32)
        grad_value_scr[target, :] = jnp.zeros((tile_len, HD), F32)
        return carry

    lax.fori_loop(0, slots, gather_slot, 0, unroll=8)
    key_scr[tail, :HD] = jnp.zeros((tail.size, HD), BF16)
    key_scr[tail, HD:] = jnp.full((tail.size, HD), HIDDEN, BF16)
    value_scr[tail, :] = jnp.zeros((tail.size, HD), BF16)
    grad_key_scr[tail, :] = jnp.zeros((tail.size, HD), F32)
    grad_value_scr[tail, :] = jnp.zeros((tail.size, HD), F32)

    def store_queries(index):
        text_rows = pl.ds(pl.multiple_of(index * span, span), span)
        return pltpu.make_async_copy(
            grad_queries_ref.at[text_rows], grad_queries_hbm.at[text_rows], out_sem.at[index]
        )

    def one_block(index, carry):
        rows = pl.ds(pl.multiple_of(index * block, block), block)
        first, steps = first_ref[index], steps_ref[index]

        def keys_of(step):
            return pl.ds(pl.multiple_of(first * tile_len + step * chunk, tile_len), chunk)

        def forward(step, carry):
            top, total, delta = carry
            where = keys_of(step)
            score = lax.dot_general(
                key_scr[where, :], queries_ref[rows, :], contract_last, preferred_element_type=F32
            )
            dprob = lax.dot_general(
                value_scr[where, :], dout_ref[rows, :], contract_last, preferred_element_type=F32
            )
            new_top = jnp.maximum(top, jnp.max(score, axis=0, keepdims=True))
            shrink = jnp.exp2((top - new_top) * rate)
            expo = jnp.exp2((score - new_top) * rate)
            expo_scr[step] = expo
            dprob_scr[step] = dprob
            top_scr[pl.ds(step, 1), :] = new_top
            return (
                new_top,
                total * shrink + jnp.sum(expo, axis=0, keepdims=True),
                delta * shrink + jnp.sum(expo * dprob, axis=0, keepdims=True),
            )

        zero = jnp.zeros((1, block), F32)
        top, total, delta = lax.fori_loop(
            0, steps, forward, (jnp.full((1, block), 2 * HIDDEN, F32), zero, zero)
        )
        inverse = 1.0 / total
        delta = delta * inverse

        def backward(step, grad_query):
            where = keys_of(step)
            factor = jnp.exp2((top_scr[pl.ds(step, 1), :] - top) * rate) * inverse
            prob = expo_scr[step] * factor
            dscore = (prob * (dprob_scr[step] - delta)).astype(BF16)
            grad_value_scr[where, :] += lax.dot_general(
                prob.astype(BF16), dout_ref[rows, :], contract_inner, preferred_element_type=F32
            )
            grad_key_scr[where, :] += lax.dot_general(
                dscore, queries_ref[rows, :HD], contract_inner, preferred_element_type=F32
            )
            return grad_query + lax.dot_general(
                dscore, key_scr[where, :HD], contract_first, preferred_element_type=F32
            )

        grad_query = lax.fori_loop(0, steps, backward, jnp.zeros((block, HD), F32))
        grad_query = (grad_query * scale).astype(BF16)
        text_rows = pl.ds(pl.multiple_of(index * span, span), span)
        for head in range(group):
            mine = grad_query[head * span : (head + 1) * span]
            grad_queries_ref[text_rows, head * HD : (head + 1) * HD] = mine
        store_queries(index).start()
        return carry

    lax.fori_loop(0, blocks, one_block, 0)

    def return_slot(slot, carry):
        source = pl.ds(holder_ref[slot] * pieces, pieces)
        rank = rank_ref[slot]
        where = pl.ds(pl.multiple_of(slot * tile_len, tile_len), tile_len)
        shape = (pieces, tile_len // pieces, HD)
        back_ref[source, rank] = (grad_key_scr[where, :] * scale).astype(BF16).reshape(shape)
        back_ref[source, capacity + rank] = grad_value_scr[where, :].astype(BF16).reshape(shape)
        return carry

    lax.fori_loop(0, slots, return_slot, 0, unroll=8)
    for index in range(blocks):
        store_queries(index).wait()


def by_block(rows, span):
    blocks = rows.reshape(rows.shape[0] // span, span, rows.shape[1] // HD, HD)
    return blocks.transpose(0, 2, 1, 3).reshape(-1, HD)


def prepare(queries, dout, tile_docs, tile_rows, doc_ends):
    rows = queries.shape[0]
    group = queries.shape[1] // HD
    docs = tile_docs[:, None] == jnp.arange(doc_ends.shape[0], dtype=jnp.int32)[None, :]
    slot_ends = jnp.sum(jnp.where(docs, doc_ends[None, :], 0), axis=1)
    slot_begins = jnp.sum(jnp.where(docs[:, 1:], doc_ends[None, :-1], 0), axis=1)
    text_row = jnp.arange(rows, dtype=jnp.int32)
    seen = (text_row[None, :] >= tile_rows[:, None]) & (text_row[None, :] < slot_ends[:, None])
    bias = jnp.where(seen, 0.0, HIDDEN).astype(F32)
    tile_len = TILE
    chunk_slots = CHUNK // tile_len
    block_begin = jnp.arange(rows * group // BLOCK, dtype=jnp.int32) * (BLOCK // group)
    first = jnp.sum((slot_ends[None, :] <= block_begin[:, None]).astype(jnp.int32), axis=1)
    until = jnp.sum(
        (slot_begins[None, :] < block_begin[:, None] + BLOCK // group).astype(jnp.int32), axis=1
    )
    steps = (until - first + chunk_slots - 1) // chunk_slots

    flat = rows * group
    span = BLOCK // group
    query_rows = by_block(queries, span)
    dout_rows = by_block(dout, span)
    position = jnp.arange(flat, dtype=jnp.int32)
    own = position // BLOCK * span + position % span
    own_row = own[:, None] == text_row[None, :]
    query_rows = jnp.concatenate([query_rows, own_row.astype(BF16)], axis=1)

    return first, steps, bias, query_rows, dout_rows


def attention(recv, holder, rank, first, steps, bias, query_rows, dout_rows):
    smem = pl.BlockSpec(memory_space=pltpu.SMEM)
    vmem = pl.BlockSpec(memory_space=pltpu.VMEM)
    slots, rows = bias.shape
    group = query_rows.shape[0] // rows
    key_count = slots * TILE
    return pl.pallas_call(
        attend_backward,
        out_shape=(
            jax.ShapeDtypeStruct(recv.shape, BF16),
            jax.ShapeDtypeStruct((rows, group * HD), BF16),
        ),
        in_specs=[smem] * 4 + [vmem] * 4,
        out_specs=(vmem, pl.BlockSpec(memory_space=pl.ANY)),
        scratch_shapes=[
            pltpu.VMEM((key_count + CHUNK, 2 * HD), BF16),
            pltpu.VMEM((key_count + CHUNK, HD), BF16),
            pltpu.VMEM((-(-key_count // CHUNK), CHUNK, BLOCK), F32),
            pltpu.VMEM((-(-key_count // CHUNK), CHUNK, BLOCK), F32),
            pltpu.VMEM((-(-key_count // CHUNK), BLOCK), F32),
            pltpu.VMEM((key_count + CHUNK, HD), F32),
            pltpu.VMEM((key_count + CHUNK, HD), F32),
            pltpu.VMEM((rows, group * HD), BF16),
            pltpu.SemaphoreType.DMA((rows * group // BLOCK,)),
        ],
        compiler_params=pltpu.CompilerParams(vmem_limit_bytes=VMEM_LIMIT),
        name="attend_backward",
    )(holder, rank, first, steps, bias, recv, query_rows, dout_rows)


def per_device(queries, keys_in, values_in, dout, req_tiles, tile_docs, tile_rows, doc_ends):
    dp_count = lax.axis_size("dp")
    heads = lax.axis_size("tensor")
    slots = req_tiles.shape[0]
    capacity = slots // dp_count + 1
    row_part = keys_in.shape[1]
    rows = queries.shape[0]
    smem = pl.BlockSpec(memory_space=pltpu.SMEM)
    vmem = pl.BlockSpec(memory_space=pltpu.VMEM)
    hbm = pl.BlockSpec(memory_space=pl.ANY)
    params = pltpu.CompilerParams(vmem_limit_bytes=VMEM_LIMIT)

    asked, rank, holder = pl.pallas_call(
        functools.partial(ask, capacity),
        out_shape=(
            jax.ShapeDtypeStruct((dp_count, HD), jnp.int32),
            jax.ShapeDtypeStruct((1, slots), jnp.int32),
            jax.ShapeDtypeStruct((1, slots), jnp.int32),
        ),
        in_specs=[vmem],
        out_specs=(vmem, vmem, vmem),
        name="ask",
    )(req_tiles.reshape(1, slots))
    holder, rank = holder.reshape(slots), rank.reshape(slots)
    asked = asked[:, None, :]
    ranks = jnp.arange(capacity, dtype=jnp.int32)[None, :, None]
    wanted = lax.all_to_all(asked, "dp", split_axis=0, concat_axis=0, tiled=True)[:, :, :capacity]

    prepared = prepare(queries, dout, tile_docs, tile_rows, doc_ends)
    tile_index = jnp.arange(slots, dtype=jnp.int32)[:, None, None]
    lines = jnp.arange(dp_count, dtype=jnp.int32)[:, None] * (heads * 2 * capacity) + ranks[:, :, 0]
    source = jnp.sum(jnp.where(wanted[:, 0][None] == tile_index, lines[None], 0), axis=(1, 2))
    wanted, prepared, source, holder, rank = lax.optimization_barrier(
        (wanted, prepared, source, holder, rank)
    )

    send = pl.pallas_call(
        pick_tiles,
        out_shape=jax.ShapeDtypeStruct((dp_count * heads, 2 * capacity, row_part, HD), BF16),
        in_specs=[smem, vmem, vmem],
        out_specs=vmem,
        compiler_params=params,
        name="pick_tiles",
    )(wanted, keys_in, values_in)
    recv = lax.all_to_all(send, ("dp", "tensor"), split_axis=0, concat_axis=0, tiled=True)

    back, grad_queries = attention(recv, holder, rank, *prepared)

    home = lax.all_to_all(back, ("dp", "tensor"), split_axis=0, concat_axis=0, tiled=True)
    grad_keys, grad_values = pl.pallas_call(
        place_tiles,
        out_shape=(
            jax.ShapeDtypeStruct(keys_in.shape, BF16),
            jax.ShapeDtypeStruct(values_in.shape, BF16),
        ),
        in_specs=[smem, vmem],
        out_specs=(hbm, hbm),
        scratch_shapes=[
            pltpu.VMEM(keys_in.shape, BF16),
            pltpu.VMEM(values_in.shape, BF16),
            pltpu.SemaphoreType.DMA((2, PARTS)),
        ],
        compiler_params=params,
        name="place_tiles",
    )(source, home)
    return (grad_queries, grad_keys, grad_values)


def solution(mesh):
    return jax.shard_map(
        per_device,
        mesh=mesh,
        in_specs=(
            P("dp", "tensor"),
            P("dp", "tensor", None),
            P("dp", "tensor", None),
            P("dp", "tensor"),
            P("dp"),
            P("dp"),
            P("dp"),
            P("dp"),
        ),
        out_specs=(P("dp", "tensor"), P("dp", "tensor", None), P("dp", "tensor", None)),
        check_vma=False,
    )
```

```python
import functools
import math

import jax
import jax.numpy as jnp
from jax import lax
from jax.experimental import pallas as pl
from jax.experimental.pallas import tpu as pltpu
from jax.sharding import PartitionSpec as P

HD = 128
TILE = 16
BF16 = jnp.bfloat16
F32 = jnp.float32
HIDDEN = -1e30
CHUNK = 768
BLOCK = 256
PARTS = 8
VMEM_LIMIT = 48 * 1024 * 1024


def ask(capacity, list_ref, asked_ref, rank_ref, holder_ref):
    holders, lanes = asked_ref.shape
    slots = list_ref.shape[1]
    tiles = list_ref[...]
    across = jnp.broadcast_to(tiles // slots, (slots, slots))
    slot_here = lax.broadcasted_iota(jnp.int32, (slots, slots), 1)
    slot_before = lax.broadcasted_iota(jnp.int32, (slots, slots), 0)
    before = (across.T == across) & (slot_before < slot_here)
    rank = jnp.sum(before.astype(jnp.int32), axis=0, keepdims=True)
    rank_ref[...] = rank
    holder_ref[...] = tiles // slots
    holder = lax.broadcasted_iota(jnp.int32, (holders, slots), 0)
    lane = lax.broadcasted_iota(jnp.int32, (holders, lanes), 1)
    asked = jnp.full((holders, lanes), -1, jnp.int32)
    for step in range(capacity):
        mine = (across[:holders] == holder) & (rank == step)
        tile = jnp.sum(jnp.where(mine, tiles % slots + 1, 0), axis=1, keepdims=True) - 1
        asked = jnp.where(lane == step, tile, asked)
    asked_ref[...] = asked


def pick_tiles(wanted_ref, keys_ref, values_ref, send_ref):
    readers, _, capacity = wanted_ref.shape
    heads = keys_ref.shape[2] // HD
    def copy_tile(reader, rank):
        tile = jnp.maximum(wanted_ref[reader, 0, rank], 0)
        for head in range(heads):
            cols = slice(head * HD, (head + 1) * HD)
            send_ref[reader * heads + head, rank] = keys_ref[tile, :, cols]
            send_ref[reader * heads + head, capacity + rank] = values_ref[tile, :, cols]

    def first_tiles(reader, carry):
        for rank in range(capacity - 1):
            copy_tile(reader, rank)
        return carry

    def last_tile(reader, carry):
        rank = capacity - 1
        pl.when(wanted_ref[reader, 0, rank] >= 0)(functools.partial(copy_tile, reader, rank))
        return carry

    lax.fori_loop(0, readers, first_tiles, 0, unroll=4)
    lax.fori_loop(0, readers, last_tile, 0, unroll=8)


def place_tiles(
    source_ref, home_ref, grad_keys_hbm, grad_values_hbm, grad_keys_ref, grad_values_ref, out_sem
):
    chunks, lines = home_ref.shape[:2]
    capacity = lines // 2
    heads = grad_keys_ref.shape[2] // HD
    flat_ref = home_ref.reshape(chunks * lines, *home_ref.shape[2:])
    part = grad_keys_ref.shape[0] // PARTS
    stores = []
    for step in range(PARTS):

        def one_tile(offset, carry):
            tile = step * part + offset
            source = source_ref[tile]
            for head in range(heads):
                cols = slice(head * HD, (head + 1) * HD)
                grad_keys_ref[tile, :, cols] = flat_ref[source + lines * head]
                grad_values_ref[tile, :, cols] = flat_ref[source + lines * head + capacity]
            return carry

        lax.fori_loop(0, part, one_tile, 0, unroll=4)
        rows = pl.ds(step * part, part)
        for kind, (ref, hbm) in enumerate(
            ((grad_keys_ref, grad_keys_hbm), (grad_values_ref, grad_values_hbm))
        ):
            stores.append(
                pltpu.make_async_copy(ref.at[rows], hbm.at[rows], out_sem.at[kind, step])
            )
            stores[-1].start()
    for store in stores:
        store.wait()


def attend_backward(
    holder_ref,
    rank_ref,
    first_ref,
    steps_ref,
    bias_ref,
    recv_ref,
    queries_ref,
    dout_ref,
    back_ref,
    grad_queries_hbm,
    key_scr,
    value_scr,
    expo_scr,
    dprob_scr,
    top_scr,
    grad_key_scr,
    grad_value_scr,
    grad_queries_ref,
    out_sem,
):
    scale = 1.0 / math.sqrt(HD)
    rate = scale * math.log2(math.e)
    slots = bias_ref.shape[0]
    capacity = recv_ref.shape[1] // 2
    tile_len = TILE
    pieces = tile_len // recv_ref.shape[2]
    chunk, block = expo_scr.shape[1:]
    blocks = queries_ref.shape[0] // block
    group = grad_queries_ref.shape[1] // HD
    span = block // group
    key_count = slots * tile_len
    tail = pl.ds(key_count, key_scr.shape[0] - key_count)
    contract_last = (((1,), (1,)), ((), ()))
    contract_inner = (((1,), (0,)), ((), ()))
    contract_first = (((0,), (0,)), ((), ()))

    def gather_slot(slot, carry):
        source = pl.ds(holder_ref[slot] * pieces, pieces)
        rank = rank_ref[slot]
        target = pl.ds(pl.multiple_of(slot * tile_len, tile_len), tile_len)
        key_scr[target, :HD] = recv_ref[source, rank].reshape(tile_len, HD)
        key_scr[target, HD:] = jnp.broadcast_to(bias_ref[pl.ds(slot, 1), :], (tile_len, HD)).astype(
            BF16
        )
        value_scr[target, :] = recv_ref[source, capacity + rank].reshape(tile_len, HD)
        grad_key_scr[target, :] = jnp.zeros((tile_len, HD), F32)
        grad_value_scr[target, :] = jnp.zeros((tile_len, HD), F32)
        return carry

    lax.fori_loop(0, slots, gather_slot, 0, unroll=8)
    key_scr[tail, :HD] = jnp.zeros((tail.size, HD), BF16)
    key_scr[tail, HD:] = jnp.full((tail.size, HD), HIDDEN, BF16)
    value_scr[tail, :] = jnp.zeros((tail.size, HD), BF16)
    grad_key_scr[tail, :] = jnp.zeros((tail.size, HD), F32)
    grad_value_scr[tail, :] = jnp.zeros((tail.size, HD), F32)

    def store_queries(index):
        text_rows = pl.ds(pl.multiple_of(index * span, span), span)
        return pltpu.make_async_copy(
            grad_queries_ref.at[text_rows], grad_queries_hbm.at[text_rows], out_sem.at[index]
        )

    def one_block(index, carry):
        rows = pl.ds(pl.multiple_of(index * block, block), block)
        first, steps = first_ref[index], steps_ref[index]

        def keys_of(step):
            return pl.ds(pl.multiple_of(first * tile_len + step * chunk, tile_len), chunk)

        def forward(step, carry):
            top, total, delta = carry
            where = keys_of(step)
            score = lax.dot_general(
                key_scr[where, :], queries_ref[rows, :], contract_last, preferred_element_type=F32
            )
            dprob = lax.dot_general(
                value_scr[where, :], dout_ref[rows, :], contract_last, preferred_element_type=F32
            )
            new_top = jnp.maximum(top, jnp.max(score, axis=0, keepdims=True))
            shrink = jnp.exp2((top - new_top) * rate)
            expo = jnp.exp2((score - new_top) * rate)
            expo_scr[step] = expo
            dprob_scr[step] = dprob
            top_scr[pl.ds(step, 1), :] = new_top
            return (
                new_top,
                total * shrink + jnp.sum(expo, axis=0, keepdims=True),
                delta * shrink + jnp.sum(expo * dprob, axis=0, keepdims=True),
            )

        zero = jnp.zeros((1, block), F32)
        top, total, delta = lax.fori_loop(
            0, steps, forward, (jnp.full((1, block), 2 * HIDDEN, F32), zero, zero)
        )
        inverse = 1.0 / total
        delta = delta * inverse

        def backward(step, grad_query):
            where = keys_of(step)
            factor = jnp.exp2((top_scr[pl.ds(step, 1), :] - top) * rate) * inverse
            prob = expo_scr[step] * factor
            dscore = (prob * (dprob_scr[step] - delta)).astype(BF16)
            grad_value_scr[where, :] += lax.dot_general(
                prob.astype(BF16), dout_ref[rows, :], contract_inner, preferred_element_type=F32
            )
            grad_key_scr[where, :] += lax.dot_general(
                dscore, queries_ref[rows, :HD], contract_inner, preferred_element_type=F32
            )
            return grad_query + lax.dot_general(
                dscore, key_scr[where, :HD], contract_first, preferred_element_type=F32
            )

        grad_query = lax.fori_loop(0, steps, backward, jnp.zeros((block, HD), F32))
        grad_query = (grad_query * scale).astype(BF16)
        text_rows = pl.ds(pl.multiple_of(index * span, span), span)
        for head in range(group):
            mine = grad_query[head * span : (head + 1) * span]
            grad_queries_ref[text_rows, head * HD : (head + 1) * HD] = mine
        store_queries(index).start()
        return carry

    lax.fori_loop(0, blocks, one_block, 0)

    def return_slot(slot, carry):
        source = pl.ds(holder_ref[slot] * pieces, pieces)
        rank = rank_ref[slot]
        where = pl.ds(pl.multiple_of(slot * tile_len, tile_len), tile_len)
        shape = (pieces, tile_len // pieces, HD)
        back_ref[source, rank] = (grad_key_scr[where, :] * scale).astype(BF16).reshape(shape)
        back_ref[source, capacity + rank] = grad_value_scr[where, :].astype(BF16).reshape(shape)
        return carry

    lax.fori_loop(0, slots, return_slot, 0, unroll=8)
    for index in range(blocks):
        store_queries(index).wait()


def by_block(rows, span):
    blocks = rows.reshape(rows.shape[0] // span, span, rows.shape[1] // HD, HD)
    return blocks.transpose(0, 2, 1, 3).reshape(-1, HD)


def prepare(queries, dout, tile_docs, tile_rows, doc_ends):
    rows = queries.shape[0]
    group = queries.shape[1] // HD
    docs = tile_docs[:, None] == jnp.arange(doc_ends.shape[0], dtype=jnp.int32)[None, :]
    slot_ends = jnp.sum(jnp.where(docs, doc_ends[None, :], 0), axis=1)
    slot_begins = jnp.sum(jnp.where(docs[:, 1:], doc_ends[None, :-1], 0), axis=1)
    text_row = jnp.arange(rows, dtype=jnp.int32)
    seen = (text_row[None, :] >= tile_rows[:, None]) & (text_row[None, :] < slot_ends[:, None])
    bias = jnp.where(seen, 0.0, HIDDEN).astype(F32)
    tile_len = TILE
    chunk_slots = CHUNK // tile_len
    block_begin = jnp.arange(rows * group // BLOCK, dtype=jnp.int32) * (BLOCK // group)
    first = jnp.sum((slot_ends[None, :] <= block_begin[:, None]).astype(jnp.int32), axis=1)
    until = jnp.sum(
        (slot_begins[None, :] < block_begin[:, None] + BLOCK // group).astype(jnp.int32), axis=1
    )
    steps = (until - first + chunk_slots - 1) // chunk_slots

    flat = rows * group
    span = BLOCK // group
    query_rows = by_block(queries, span)
    dout_rows = by_block(dout, span)
    position = jnp.arange(flat, dtype=jnp.int32)
    own = position // BLOCK * span + position % span
    own_row = own[:, None] == text_row[None, :]
    query_rows = jnp.concatenate([query_rows, own_row.astype(BF16)], axis=1)

    return first, steps, bias, query_rows, dout_rows


def attention(recv, holder, rank, first, steps, bias, query_rows, dout_rows):
    smem = pl.BlockSpec(memory_space=pltpu.SMEM)
    vmem = pl.BlockSpec(memory_space=pltpu.VMEM)
    slots, rows = bias.shape
    group = query_rows.shape[0] // rows
    key_count = slots * TILE
    return pl.pallas_call(
        attend_backward,
        out_shape=(
            jax.ShapeDtypeStruct(recv.shape, BF16),
            jax.ShapeDtypeStruct((rows, group * HD), BF16),
        ),
        in_specs=[smem] * 4 + [vmem] * 4,
        out_specs=(vmem, pl.BlockSpec(memory_space=pl.ANY)),
        scratch_shapes=[
            pltpu.VMEM((key_count + CHUNK, 2 * HD), BF16),
            pltpu.VMEM((key_count + CHUNK, HD), BF16),
            pltpu.VMEM((-(-key_count // CHUNK), CHUNK, BLOCK), F32),
            pltpu.VMEM((-(-key_count // CHUNK), CHUNK, BLOCK), F32),
            pltpu.VMEM((-(-key_count // CHUNK), BLOCK), F32),
            pltpu.VMEM((key_count + CHUNK, HD), F32),
            pltpu.VMEM((key_count + CHUNK, HD), F32),
            pltpu.VMEM((rows, group * HD), BF16),
            pltpu.SemaphoreType.DMA((rows * group // BLOCK,)),
        ],
        compiler_params=pltpu.CompilerParams(vmem_limit_bytes=VMEM_LIMIT),
        name="attend_backward",
    )(holder, rank, first, steps, bias, recv, query_rows, dout_rows)


def per_device(queries, keys_in, values_in, dout, req_tiles, tile_docs, tile_rows, doc_ends):
    dp_count = lax.axis_size("dp")
    heads = lax.axis_size("tensor")
    slots = req_tiles.shape[0]
    capacity = slots // dp_count + 1
    row_part = keys_in.shape[1]
    rows = queries.shape[0]
    smem = pl.BlockSpec(memory_space=pltpu.SMEM)
    vmem = pl.BlockSpec(memory_space=pltpu.VMEM)
    hbm = pl.BlockSpec(memory_space=pl.ANY)
    params = pltpu.CompilerParams(vmem_limit_bytes=VMEM_LIMIT)

    asked, rank, holder = pl.pallas_call(
        functools.partial(ask, capacity),
        out_shape=(
            jax.ShapeDtypeStruct((dp_count, HD), jnp.int32),
            jax.ShapeDtypeStruct((1, slots), jnp.int32),
            jax.ShapeDtypeStruct((1, slots), jnp.int32),
        ),
        in_specs=[vmem],
        out_specs=(vmem, vmem, vmem),
        name="ask",
    )(req_tiles.reshape(1, slots))
    holder, rank = holder.reshape(slots), rank.reshape(slots)
    asked = asked[:, None, :]
    ranks = jnp.arange(capacity, dtype=jnp.int32)[None, :, None]
    wanted = lax.all_to_all(asked, "dp", split_axis=0, concat_axis=0, tiled=True)[:, :, :capacity]

    prepared = prepare(queries, dout, tile_docs, tile_rows, doc_ends)
    tile_index = jnp.arange(slots, dtype=jnp.int32)[:, None, None]
    lines = jnp.arange(dp_count, dtype=jnp.int32)[:, None] * (heads * 2 * capacity) + ranks[:, :, 0]
    source = jnp.sum(jnp.where(wanted[:, 0][None] == tile_index, lines[None], 0), axis=(1, 2))
    wanted, prepared, source, holder, rank = lax.optimization_barrier(
        (wanted, prepared, source, holder, rank)
    )

    send = pl.pallas_call(
        pick_tiles,
        out_shape=jax.ShapeDtypeStruct((dp_count * heads, 2 * capacity, row_part, HD), BF16),
        in_specs=[smem, vmem, vmem],
        out_specs=vmem,
        compiler_params=params,
        name="pick_tiles",
    )(wanted, keys_in, values_in)
    recv = lax.all_to_all(send, ("dp", "tensor"), split_axis=0, concat_axis=0, tiled=True)

    back, grad_queries = attention(recv, holder, rank, *prepared)

    home = lax.all_to_all(back, ("dp", "tensor"), split_axis=0, concat_axis=0, tiled=True)
    grad_keys, grad_values = pl.pallas_call(
        place_tiles,
        out_shape=(
            jax.ShapeDtypeStruct(keys_in.shape, BF16),
            jax.ShapeDtypeStruct(values_in.shape, BF16),
        ),
        in_specs=[smem, vmem],
        out_specs=(hbm, hbm),
        scratch_shapes=[
            pltpu.VMEM(keys_in.shape, BF16),
            pltpu.VMEM(values_in.shape, BF16),
            pltpu.SemaphoreType.DMA((2, PARTS)),
        ],
        compiler_params=params,
        name="place_tiles",
    )(source, home)
    return (grad_queries, grad_keys, grad_values)


def solution(mesh):
    return jax.shard_map(
        per_device,
        mesh=mesh,
        in_specs=(
            P("dp", "tensor"),
            P("dp", "tensor", None),
            P("dp", "tensor", None),
            P("dp", "tensor"),
            P("dp"),
            P("dp"),
            P("dp"),
            P("dp"),
        ),
        out_specs=(P("dp", "tensor"), P("dp", "tensor", None), P("dp", "tensor", None)),
        check_vma=False,
    )
```

```python
import functools
import math

import jax
import jax.numpy as jnp
from jax import lax
from jax.experimental import pallas as pl
from jax.experimental.pallas import tpu as pltpu
from jax.sharding import PartitionSpec as P

HD = 128
TILE = 16
BF16 = jnp.bfloat16
F32 = jnp.float32
HIDDEN = -1e30
CHUNK = 768
BLOCK = 256
PARTS = 8
VMEM_LIMIT = 48 * 1024 * 1024


def ask(capacity, list_ref, asked_ref, rank_ref, holder_ref):
    holders, lanes = asked_ref.shape
    slots = list_ref.shape[1]
    tiles = list_ref[...]
    across = jnp.broadcast_to(tiles // slots, (slots, slots))
    slot_here = lax.broadcasted_iota(jnp.int32, (slots, slots), 1)
    slot_before = lax.broadcasted_iota(jnp.int32, (slots, slots), 0)
    before = (across.T == across) & (slot_before < slot_here)
    rank = jnp.sum(before.astype(jnp.int32), axis=0, keepdims=True)
    rank_ref[...] = rank
    holder_ref[...] = tiles // slots
    holder = lax.broadcasted_iota(jnp.int32, (holders, slots), 0)
    lane = lax.broadcasted_iota(jnp.int32, (holders, lanes), 1)
    asked = jnp.full((holders, lanes), -1, jnp.int32)
    for step in range(capacity):
        mine = (across[:holders] == holder) & (rank == step)
        tile = jnp.sum(jnp.where(mine, tiles % slots + 1, 0), axis=1, keepdims=True) - 1
        asked = jnp.where(lane == step, tile, asked)
    asked_ref[...] = asked


def pick_tiles(wanted_ref, keys_ref, values_ref, send_ref):
    readers, _, capacity = wanted_ref.shape
    heads = keys_ref.shape[2] // HD
    def one_reader(reader, carry):
        for rank in range(capacity):
            tile = jnp.maximum(wanted_ref[reader, 0, rank], 0)
            for head in range(heads):
                cols = slice(head * HD, (head + 1) * HD)
                send_ref[reader * heads + head, rank] = keys_ref[tile, :, cols]
                send_ref[reader * heads + head, capacity + rank] = values_ref[tile, :, cols]
        return carry

    lax.fori_loop(0, readers, one_reader, 0, unroll=8)


def place_tiles(
    source_ref, home_ref, grad_keys_hbm, grad_values_hbm, grad_keys_ref, grad_values_ref, out_sem
):
    chunks, lines = home_ref.shape[:2]
    capacity = lines // 2
    heads = grad_keys_ref.shape[2] // HD
    flat_ref = home_ref.reshape(chunks * lines, *home_ref.shape[2:])
    part = grad_keys_ref.shape[0] // PARTS
    stores = []
    for step in range(PARTS):

        def one_tile(offset, carry):
            tile = step * part + offset
            source = source_ref[tile]
            for head in range(heads):
                cols = slice(head * HD, (head + 1) * HD)
                grad_keys_ref[tile, :, cols] = flat_ref[source + lines * head]
                grad_values_ref[tile, :, cols] = flat_ref[source + lines * head + capacity]
            return carry

        lax.fori_loop(0, part, one_tile, 0, unroll=4)
        rows = pl.ds(step * part, part)
        for kind, (ref, hbm) in enumerate(
            ((grad_keys_ref, grad_keys_hbm), (grad_values_ref, grad_values_hbm))
        ):
            stores.append(
                pltpu.make_async_copy(ref.at[rows], hbm.at[rows], out_sem.at[kind, step])
            )
            stores[-1].start()
    for store in stores:
        store.wait()


def attend_backward(
    holder_ref,
    rank_ref,
    first_ref,
    steps_ref,
    bias_ref,
    recv_ref,
    queries_ref,
    dout_ref,
    back_ref,
    grad_queries_hbm,
    key_scr,
    value_scr,
    expo_scr,
    dprob_scr,
    top_scr,
    grad_key_scr,
    grad_value_scr,
    grad_queries_ref,
    out_sem,
):
    scale = 1.0 / math.sqrt(HD)
    rate = scale * math.log2(math.e)
    slots = bias_ref.shape[0]
    capacity = recv_ref.shape[1] // 2
    tile_len = TILE
    pieces = tile_len // recv_ref.shape[2]
    chunk, block = expo_scr.shape[1:]
    blocks = queries_ref.shape[0] // block
    group = grad_queries_ref.shape[1] // HD
    span = block // group
    key_count = slots * tile_len
    tail = pl.ds(key_count, key_scr.shape[0] - key_count)
    contract_last = (((1,), (1,)), ((), ()))
    contract_inner = (((1,), (0,)), ((), ()))
    contract_first = (((0,), (0,)), ((), ()))

    def gather_slot(slot, carry):
        source = pl.ds(holder_ref[slot] * pieces, pieces)
        rank = rank_ref[slot]
        target = pl.ds(pl.multiple_of(slot * tile_len, tile_len), tile_len)
        key_scr[target, :HD] = recv_ref[source, rank].reshape(tile_len, HD)
        key_scr[target, HD:] = jnp.broadcast_to(bias_ref[pl.ds(slot, 1), :], (tile_len, HD)).astype(
            BF16
        )
        value_scr[target, :] = recv_ref[source, capacity + rank].reshape(tile_len, HD)
        grad_key_scr[target, :] = jnp.zeros((tile_len, HD), F32)
        grad_value_scr[target, :] = jnp.zeros((tile_len, HD), F32)
        return carry

    lax.fori_loop(0, slots, gather_slot, 0, unroll=16)
    key_scr[tail, :HD] = jnp.zeros((tail.size, HD), BF16)
    key_scr[tail, HD:] = jnp.full((tail.size, HD), HIDDEN, BF16)
    value_scr[tail, :] = jnp.zeros((tail.size, HD), BF16)
    grad_key_scr[tail, :] = jnp.zeros((tail.size, HD), F32)
    grad_value_scr[tail, :] = jnp.zeros((tail.size, HD), F32)

    def store_queries(index):
        text_rows = pl.ds(pl.multiple_of(index * span, span), span)
        return pltpu.make_async_copy(
            grad_queries_ref.at[text_rows], grad_queries_hbm.at[text_rows], out_sem.at[index]
        )

    def one_block(index, carry):
        rows = pl.ds(pl.multiple_of(index * block, block), block)
        first, steps = first_ref[index], steps_ref[index]

        def keys_of(step):
            return pl.ds(pl.multiple_of(first * tile_len + step * chunk, tile_len), chunk)

        def forward(step, carry):
            top, total, delta = carry
            where = keys_of(step)
            score = lax.dot_general(
                key_scr[where, :], queries_ref[rows, :], contract_last, preferred_element_type=F32
            )
            dprob = lax.dot_general(
                value_scr[where, :], dout_ref[rows, :], contract_last, preferred_element_type=F32
            )
            new_top = jnp.maximum(top, jnp.max(score, axis=0, keepdims=True))
            shrink = jnp.exp2((top - new_top) * rate)
            expo = jnp.exp2((score - new_top) * rate)
            expo_scr[step] = expo
            dprob_scr[step] = dprob
            top_scr[pl.ds(step, 1), :] = new_top
            return (
                new_top,
                total * shrink + jnp.sum(expo, axis=0, keepdims=True),
                delta * shrink + jnp.sum(expo * dprob, axis=0, keepdims=True),
            )

        zero = jnp.zeros((1, block), F32)
        top, total, delta = lax.fori_loop(
            0, steps, forward, (jnp.full((1, block), 2 * HIDDEN, F32), zero, zero)
        )
        inverse = 1.0 / total
        delta = delta * inverse

        def backward(step, grad_query):
            where = keys_of(step)
            factor = jnp.exp2((top_scr[pl.ds(step, 1), :] - top) * rate) * inverse
            prob = expo_scr[step] * factor
            dscore = (prob * (dprob_scr[step] - delta)).astype(BF16)
            grad_value_scr[where, :] += lax.dot_general(
                prob.astype(BF16), dout_ref[rows, :], contract_inner, preferred_element_type=F32
            )
            grad_key_scr[where, :] += lax.dot_general(
                dscore, queries_ref[rows, :HD], contract_inner, preferred_element_type=F32
            )
            return grad_query + lax.dot_general(
                dscore, key_scr[where, :HD], contract_first, preferred_element_type=F32
            )

        grad_query = lax.fori_loop(0, steps, backward, jnp.zeros((block, HD), F32))
        grad_query = (grad_query * scale).astype(BF16)
        text_rows = pl.ds(pl.multiple_of(index * span, span), span)
        for head in range(group):
            mine = grad_query[head * span : (head + 1) * span]
            grad_queries_ref[text_rows, head * HD : (head + 1) * HD] = mine
        store_queries(index).start()
        return carry

    lax.fori_loop(0, blocks, one_block, 0)

    def return_slot(slot, carry):
        source = pl.ds(holder_ref[slot] * pieces, pieces)
        rank = rank_ref[slot]
        where = pl.ds(pl.multiple_of(slot * tile_len, tile_len), tile_len)
        shape = (pieces, tile_len // pieces, HD)
        back_ref[source, rank] = (grad_key_scr[where, :] * scale).astype(BF16).reshape(shape)
        back_ref[source, capacity + rank] = grad_value_scr[where, :].astype(BF16).reshape(shape)
        return carry

    lax.fori_loop(0, slots, return_slot, 0, unroll=16)
    for index in range(blocks):
        store_queries(index).wait()


def by_block(rows, span):
    blocks = rows.reshape(rows.shape[0] // span, span, rows.shape[1] // HD, HD)
    return blocks.transpose(0, 2, 1, 3).reshape(-1, HD)


def prepare(queries, dout, tile_docs, tile_rows, doc_ends):
    rows = queries.shape[0]
    group = queries.shape[1] // HD
    docs = tile_docs[:, None] == jnp.arange(doc_ends.shape[0], dtype=jnp.int32)[None, :]
    slot_ends = jnp.sum(jnp.where(docs, doc_ends[None, :], 0), axis=1)
    slot_begins = jnp.sum(jnp.where(docs[:, 1:], doc_ends[None, :-1], 0), axis=1)
    text_row = jnp.arange(rows, dtype=jnp.int32)
    seen = (text_row[None, :] >= tile_rows[:, None]) & (text_row[None, :] < slot_ends[:, None])
    bias = jnp.where(seen, 0.0, HIDDEN).astype(F32)
    tile_len = TILE
    chunk_slots = CHUNK // tile_len
    block_begin = jnp.arange(rows * group // BLOCK, dtype=jnp.int32) * (BLOCK // group)
    first = jnp.sum((slot_ends[None, :] <= block_begin[:, None]).astype(jnp.int32), axis=1)
    until = jnp.sum(
        (slot_begins[None, :] < block_begin[:, None] + BLOCK // group).astype(jnp.int32), axis=1
    )
    steps = (until - first + chunk_slots - 1) // chunk_slots

    flat = rows * group
    span = BLOCK // group
    query_rows = by_block(queries, span)
    dout_rows = by_block(dout, span)
    position = jnp.arange(flat, dtype=jnp.int32)
    own = position // BLOCK * span + position % span
    own_row = own[:, None] == text_row[None, :]
    query_rows = jnp.concatenate([query_rows, own_row.astype(BF16)], axis=1)

    return first, steps, bias, query_rows, dout_rows


def attention(recv, holder, rank, first, steps, bias, query_rows, dout_rows):
    smem = pl.BlockSpec(memory_space=pltpu.SMEM)
    vmem = pl.BlockSpec(memory_space=pltpu.VMEM)
    slots, rows = bias.shape
    group = query_rows.shape[0] // rows
    key_count = slots * TILE
    return pl.pallas_call(
        attend_backward,
        out_shape=(
            jax.ShapeDtypeStruct(recv.shape, BF16),
            jax.ShapeDtypeStruct((rows, group * HD), BF16),
        ),
        in_specs=[smem] * 4 + [vmem] * 4,
        out_specs=(vmem, pl.BlockSpec(memory_space=pl.ANY)),
        scratch_shapes=[
            pltpu.VMEM((key_count + CHUNK, 2 * HD), BF16),
            pltpu.VMEM((key_count + CHUNK, HD), BF16),
            pltpu.VMEM((-(-key_count // CHUNK), CHUNK, BLOCK), F32),
            pltpu.VMEM((-(-key_count // CHUNK), CHUNK, BLOCK), F32),
            pltpu.VMEM((-(-key_count // CHUNK), BLOCK), F32),
            pltpu.VMEM((key_count + CHUNK, HD), F32),
            pltpu.VMEM((key_count + CHUNK, HD), F32),
            pltpu.VMEM((rows, group * HD), BF16),
            pltpu.SemaphoreType.DMA((rows * group // BLOCK,)),
        ],
        compiler_params=pltpu.CompilerParams(vmem_limit_bytes=VMEM_LIMIT),
        name="attend_backward",
    )(holder, rank, first, steps, bias, recv, query_rows, dout_rows)


def per_device(queries, keys_in, values_in, dout, req_tiles, tile_docs, tile_rows, doc_ends):
    dp_count = lax.axis_size("dp")
    heads = lax.axis_size("tensor")
    slots = req_tiles.shape[0]
    capacity = slots // dp_count + 1
    row_part = keys_in.shape[1]
    rows = queries.shape[0]
    smem = pl.BlockSpec(memory_space=pltpu.SMEM)
    vmem = pl.BlockSpec(memory_space=pltpu.VMEM)
    hbm = pl.BlockSpec(memory_space=pl.ANY)
    params = pltpu.CompilerParams(vmem_limit_bytes=VMEM_LIMIT)

    asked, rank, holder = pl.pallas_call(
        functools.partial(ask, capacity),
        out_shape=(
            jax.ShapeDtypeStruct((dp_count, HD), jnp.int32),
            jax.ShapeDtypeStruct((1, slots), jnp.int32),
            jax.ShapeDtypeStruct((1, slots), jnp.int32),
        ),
        in_specs=[vmem],
        out_specs=(vmem, vmem, vmem),
        name="ask",
    )(req_tiles.reshape(1, slots))
    holder, rank = holder.reshape(slots), rank.reshape(slots)
    asked = asked[:, None, :]
    ranks = jnp.arange(capacity, dtype=jnp.int32)[None, :, None]
    wanted = lax.all_to_all(asked, "dp", split_axis=0, concat_axis=0, tiled=True)[:, :, :capacity]

    prepared = prepare(queries, dout, tile_docs, tile_rows, doc_ends)
    tile_index = jnp.arange(slots, dtype=jnp.int32)[:, None, None]
    lines = jnp.arange(dp_count, dtype=jnp.int32)[:, None] * (heads * 2 * capacity) + ranks[:, :, 0]
    source = jnp.sum(jnp.where(wanted[:, 0][None] == tile_index, lines[None], 0), axis=(1, 2))
    wanted, prepared, source, holder, rank = lax.optimization_barrier(
        (wanted, prepared, source, holder, rank)
    )

    send = pl.pallas_call(
        pick_tiles,
        out_shape=jax.ShapeDtypeStruct((dp_count * heads, 2 * capacity, row_part, HD), BF16),
        in_specs=[smem, vmem, vmem],
        out_specs=vmem,
        compiler_params=params,
        name="pick_tiles",
    )(wanted, keys_in, values_in)
    recv = lax.all_to_all(send, ("dp", "tensor"), split_axis=0, concat_axis=0, tiled=True)

    back, grad_queries = attention(recv, holder, rank, *prepared)

    home = lax.all_to_all(back, ("dp", "tensor"), split_axis=0, concat_axis=0, tiled=True)
    grad_keys, grad_values = pl.pallas_call(
        place_tiles,
        out_shape=(
            jax.ShapeDtypeStruct(keys_in.shape, BF16),
            jax.ShapeDtypeStruct(values_in.shape, BF16),
        ),
        in_specs=[smem, vmem],
        out_specs=(hbm, hbm),
        scratch_shapes=[
            pltpu.VMEM(keys_in.shape, BF16),
            pltpu.VMEM(values_in.shape, BF16),
            pltpu.SemaphoreType.DMA((2, PARTS)),
        ],
        compiler_params=params,
        name="place_tiles",
    )(source, home)
    return (grad_queries, grad_keys, grad_values)


def solution(mesh):
    return jax.shard_map(
        per_device,
        mesh=mesh,
        in_specs=(
            P("dp", "tensor"),
            P("dp", "tensor", None),
            P("dp", "tensor", None),
            P("dp", "tensor"),
            P("dp"),
            P("dp"),
            P("dp"),
            P("dp"),
        ),
        out_specs=(P("dp", "tensor"), P("dp", "tensor", None), P("dp", "tensor", None)),
        check_vma=False,
    )
```
